256 devices in a mesh: dp: 16 (over z, core), tensor: 16 (over y, x).
Axes of the slice: x: 4, y: 4, z: 8, core: 2. Of those that a mesh axis runs over, the one named last changes fastest.
Arguments:
- grads: bfloat16 [16, 4096, 14336], P('dp', 'tensor'), as said below
- basis: float32 [4096, 512], P('tensor'), as said below
- weight: float32 [4096, 14336], P('tensor', 'dp'), may hold values from -6 to 6
- first_moment: float32 [512, 14336], P('tensor', 'dp'), may hold values from -0.6 to 0.6
- second_moment: float32 [512, 14336], P('tensor', 'dp'), may hold values from 0.01 to 0.1
Outputs:
- new_weight: float32 [4096, 14336], P('tensor', 'dp')
- new_first: float32 [512, 14336], P('tensor', 'dp')
- new_second: float32 [512, 14336], P('tensor', 'dp')
The draws below stay inside these ranges and needn't reach their ends.
Inputs may be any that keep to these rules, and one draw needn't show every extreme that they name: `grads`: each member's gradient: entries of order tens, with magnitudes up to some 2,600. A dense basis with entries of order 1 / sqrt(4096).
All inputs are finite; a program needn't handle non-finite values.
Results may differ from the reference program's by a relative error of at most 0.0003.
Values sent between devices are 32-bit elements; how exact they have to be, the bound alone decides.
A program may use at most 128 MiB of HBM per device.

```python
import math
import jax
import jax.numpy as jnp
from jax import lax

DW = 4096
FFW = 14336
R = 512
STEP = 10
MEMBERS = 16
N_DP = 16


def profile(key, count, rise):
    spread = jax.random.uniform(key, (count,), jnp.float32)
    place = jnp.arange(count, dtype=jnp.float32) / count
    return rise ** place * 10.0 ** spread


def basis_normal(key):
    return jnp.clip(jax.random.normal(jax.random.fold_in(key, 5), (DW, R), jnp.float32), -5.0, 5.0)


def draw_grads(key, part):
    shared = basis_normal(key)
    key = jax.random.fold_in(key, 11)
    key_cols = jax.random.fold_in(key, 0)
    key_rows = jax.random.fold_in(key, 1)
    key_base = jax.random.fold_in(key, 2)
    key_pick = jax.random.fold_in(key, 4)
    key_along = jax.random.fold_in(key, 5)
    columns = profile(key_cols, FFW, 3.0)
    rows_scale = profile(key_rows, DW, 1.0)
    pick = jax.random.randint(key_pick, (), 0, R)
    base = jnp.clip(jax.random.normal(key_base, (N_DP, DW, FFW), jnp.float32), -5.0, 5.0)
    leading = lax.dynamic_index_in_dim(shared, pick, 1, keepdims=False)
    along = jnp.clip(jax.random.normal(key_along, (FFW,), jnp.float32), -5.0, 5.0)
    base = base + 0.15 * leading[None, :, None] * along[None, None, :]
    return (base * rows_scale[None, :, None] * columns[None, None, :]).astype(jnp.bfloat16)


def draw_basis(key, part):
    shared = basis_normal(key)
    rise = 3.0 ** (jnp.arange(R, dtype=jnp.float32) / R)
    return shared * rise[None, :] / DW ** 0.5


def level_of(stream_key, extent, pieces, least, top_value):
    level, own = 1.0, jax.random.fold_in(stream_key, 6)
    for dim, parts in pieces:
        steps = jnp.exp(jax.random.uniform(jax.random.fold_in(own, dim), (parts,), jnp.float32, least / len(pieces), top_value / len(pieces)))
        level = level * jnp.repeat(steps, extent[dim] // parts).reshape([-1 if axis == dim else 1 for axis in range(len(extent))])
    return level


def centred(stream_key, shape, deviation, most, pieces=(), kind=jnp.bfloat16):
    result = deviation * jax.random.normal(stream_key, shape, jnp.float32)
    if pieces:
        result = result * level_of(stream_key, shape, pieces, -0.22, 0.18)
    return jnp.clip(result, -most, most).astype(kind)


def setup_inputs(seed: int = 0) -> dict:
    seeds = jax.random.split(jax.random.key(seed), 6)
    grads = draw_grads(jax.random.fold_in(seeds[5], 71), 0)
    basis = draw_basis(jax.random.fold_in(seeds[5], 71), 0)
    weight = centred(seeds[2], (DW, FFW), 1.0, 6.0, ((0, 16), (1, 16)), jnp.float32)
    first_moment = centred(seeds[3], (R, FFW), 0.1, 0.6, ((0, 16), (1, 16)), jnp.float32)
    second_moment = jnp.clip(jnp.exp(math.log(0.1) - 2.3025851 * jax.random.uniform(seeds[4], (R, FFW), jnp.float32) ** level_of(seeds[4], (R, FFW), ((0, 16), (1, 16)), -0.2, 0.2)), 0.01, 0.1)
    return {"grads": grads, "basis": basis, "weight": weight, "first_moment": first_moment, "second_moment": second_moment}


def reference(grads, basis, weight, first_moment, second_moment):

    def add_member(index, total):
        member = lax.dynamic_index_in_dim(grads, index, 0, keepdims=False)
        return total + member.astype(jnp.float32)
    reduced = lax.fori_loop(0, MEMBERS, add_member, jnp.zeros((DW, FFW), jnp.float32))
    projected = jnp.dot(basis.T, reduced, precision=lax.Precision.HIGHEST, preferred_element_type=jnp.float32)
    norm = jnp.sqrt(jnp.sum(projected * projected))
    limit = 0.25 * (R * FFW) ** 0.5
    factor = jnp.minimum(jnp.float32(1.0), limit / (norm + 1e-06))
    clipped = factor * projected
    new_first = 0.9 * first_moment + 0.1 * clipped
    new_second = 0.95 * second_moment + 0.05 * clipped * clipped
    direction = new_first / (1.0 - 0.9 ** STEP) / (jnp.sqrt(new_second / (1.0 - 0.95 ** STEP)) + 1e-08)
    delta = jnp.dot(basis, direction, precision=lax.Precision.HIGHEST, preferred_element_type=jnp.float32)
    new_weight = weight - 0.5 * delta
    return (new_weight, new_first, new_second)
```

```python
import jax
import jax.numpy as jnp
from jax import lax
from jax.experimental import pallas as pl
from jax.experimental.pallas import tpu as pltpu
from jax.sharding import PartitionSpec as P

FFW = 14336
R = 512
STEP = 10
OWN = 896
LANE = 128
ROWS = 256
NZ = 8
NA = 4
NB = 3
MESH = pl.DeviceIdType.MESH
F32 = jnp.float32
BF16 = jnp.bfloat16


def split(x):
    hi = x.astype(BF16)
    return hi, (x - hi.astype(F32)).astype(BF16)


def dot3(ah, al, bh, bl):
    def mm(a, b):
        return jnp.dot(a, b, preferred_element_type=F32)

    return mm(ah, bh) + (mm(ah, bl) + mm(al, bh))


def kernel(
    g_ref, basis_ref, weight_ref, first_ref, second_ref,
    out_ref, out_first_ref, out_second_ref,
    ga, gb, cs, cr, zr, pb, rb1, rb2, rb3, rb4, qr, pa, ar,
    fin, ssq1, ssq2, dirs, wbuf, m1, m2, bbuf, bth, btl, bh, bl,
    gsem, lsem, csend, crecv, zsend, zrecv, asend, arecv,
    bsend, brecv, qsend, qrecv, nsend, nrecv, dsend, drecv,
):
    d = lax.axis_index("dp")
    t = lax.axis_index("tensor")
    z, c = d // 2, d % 2
    y, x = t // 4, t % 4

    def at_z(k):
        return (((z + k + NZ) % NZ) * 2 + c, t)

    def at_x(k):
        return (d, y * 4 + (x + k + 4) % 4)

    def at_y(k):
        return (d, ((y + k + 4) % 4) * 4 + x)

    partner = (z * 2 + 1 - c, t)

    def gload(group, which, start):
        core = c if which == 0 else 1 - c
        if group < 2:
            buf, lo, width = ga.at[which, group], 256 * group, 256
        else:
            buf, lo, width = gb.at[which], NA * LANE, NB * LANE
        sem = gsem.at[group, which]
        if not start:
            pltpu.make_async_copy(buf, buf, sem).wait()
            return

        def one(k, _):
            col = pl.multiple_of(OWN * (2 * k + core) + lo, LANE)
            pltpu.make_async_copy(g_ref.at[:, pl.ds(col, width)], buf.at[k], sem).start()
            return 0

        lax.fori_loop(0, NZ, one, 0)

    small = [
        pltpu.make_async_copy(basis_ref, bbuf, lsem.at[0]),
        pltpu.make_async_copy(first_ref, m1, lsem.at[1]),
        pltpu.make_async_copy(second_ref, m2, lsem.at[2]),
        pltpu.make_async_copy(weight_ref, wbuf, lsem.at[3]),
    ]
    gload(0, 1, True)
    gload(0, 0, True)
    small[0].start()
    gload(2, 1, True)
    gload(2, 0, True)
    gload(1, 1, True)
    gload(1, 0, True)
    for cp in small[1:]:
        cp.start()

    barrier = pltpu.get_barrier_semaphore()

    def greet(k, _):
        pl.semaphore_signal(barrier, 1, device_id=((d + k) % 16, t), device_id_type=MESH)
        pl.semaphore_signal(barrier, 1, device_id=(d, (t + k) % 16), device_id_type=MESH)
        return 0

    lax.fori_loop(1, 16, greet, 0)

    pending = []

    def remote(src, dst, ssem, rsem, dev):
        cp = pltpu.make_async_remote_copy(
            src_ref=src, dst_ref=dst, send_sem=ssem, recv_sem=rsem,
            device_id=dev, device_id_type=MESH,
        )
        cp.start()
        pending.append(cp)
        return cp

    loaded = set()

    def grad(j, which, k):
        if j < NA:
            return ga[which, j // 2, k, :, (j % 2) * LANE:(j % 2 + 1) * LANE].astype(F32)
        return gb[which, k, :, (j - NA) * LANE:(j - NA + 1) * LANE].astype(F32)

    def need(j, which):
        group = j // 2 if j < NA else 2
        if (group, which) not in loaded:
            loaded.add((group, which))
            gload(group, which, False)

    core = {}

    def cast(j):
        need(j, 1)

        def one(k, _):
            cs[j, k] = grad(j, 1, k)
            return 0

        lax.fori_loop(0, NZ, one, 0)

    def exchange(j):
        core[j] = remote(cs.at[j], cr.at[j], csend.at[j], crecv.at[j], partner)

    def stage(j):
        cast(j)
        exchange(j)

    def block(k):
        return (z + k + 2 * NZ) % NZ

    az = {}

    def a_send(j, s):
        if s == 1:
            far = block(4)
            az[j, 0, 1] = remote(
                cr.at[j, far, 0:128], zr.at[j, 0, 0, 0:128],
                zsend.at[j, 0, 0], zrecv.at[j, 0, 0], at_z(1))
            az[j, 1, 1] = remote(
                cr.at[j, far, 128:256], zr.at[j, 1, 0, 0:128],
                zsend.at[j, 1, 0], zrecv.at[j, 1, 0], at_z(-1))
            return
        for side, sign in ((0, 1), (1, -1)):
            dest = block(sign * (5 - s))
            az[j, side, s - 1].wait_recv()
            if s == 2:
                rows = pl.ds(128 * side, 128)
                cr[j, dest, rows] = cr[j, dest, rows] + zr[j, side, 0, 0:128]
            else:
                cr[j, dest] = cr[j, dest] + zr[j, side, s - 2]
            az[j, side, s] = remote(
                cr.at[j, dest], zr.at[j, side, s - 1],
                zsend.at[j, side, s - 1], zrecv.at[j, side, s - 1], at_z(sign))

    def a1(j):
        need(j, 0)
        core[j].wait_recv()

        def one(k, _):
            cr[j, k] = cr[j, k] + grad(j, 0, k)
            return 0

        lax.fori_loop(0, NZ, one, 0)
        a_send(j, 1)

    def a5(j):
        az[j, 0, 4].wait_recv()
        az[j, 1, 4].wait_recv()
        total = cr[j, z] + zr[j, 0, 3] + zr[j, 1, 3]
        hi, lo = split(total)
        pa[j] = dot3(bth[...], btl[...], hi, lo).reshape(16, 32, LANE)

        def one(k, _):
            to = (t + k) % 16
            pltpu.make_async_remote_copy(
                src_ref=pa.at[j, to], dst_ref=ar.at[j, k - 1],
                send_sem=asend.at[j], recv_sem=arecv.at[j],
                device_id=(d, to), device_id_type=MESH).start()
            return 0

        lax.fori_loop(1, 16, one, 0)

    def wait_bytes(ref, sem):
        pltpu.make_async_copy(ref, ref, sem).wait()

    def a6(j):
        wait_bytes(ar.at[j], arecv.at[j])
        fin[:, j * LANE:(j + 1) * LANE] = pa[j, t] + jnp.sum(ar[j], axis=0)

    bx = {}

    def piece(j, h, stage_no, k, cols):
        lane = pl.ds(512 * h + cols[0], cols[1])
        if stage_no == 0:
            if h == 0:
                return pb.at[j, :, (x + k + 4) % 4, :, lane]
            return pb.at[j, (y + k + 4) % 4, :, :, lane]
        if h == 0:
            return pb.at[j, (y + k + 4) % 4, x, :, lane]
        return pb.at[j, y, (x + k + 4) % 4, :, lane]

    def toward(h, stage_no, k):
        return at_x(k) if (h + stage_no) % 2 == 0 else at_y(k)

    def b_first(j, stage_no):
        buf = rb1 if stage_no == 0 else rb3
        for h in (0, 1):
            for side, sign in ((0, 1), (1, -1)):
                bx[j, h, side, stage_no, 0] = remote(
                    piece(j, h, stage_no, 2, (256 * side, 256)), buf.at[j, h, side],
                    bsend.at[j, h, side, 2 * stage_no], brecv.at[j, h, side, 2 * stage_no],
                    toward(h, stage_no, sign))

    def b_second(j, stage_no):
        got, buf = (rb1, rb2) if stage_no == 0 else (rb3, rb4)
        for h in (0, 1):
            for side, sign in ((0, 1), (1, -1)):
                bx[j, h, side, stage_no, 0].wait_recv()
                part = piece(j, h, stage_no, sign, (256 * side, 256))
                part[...] = part[...] + got[j, h, side]
                bx[j, h, side, stage_no, 1] = remote(
                    piece(j, h, stage_no, sign, (0, 512)), buf.at[j, h, side],
                    bsend.at[j, h, side, 2 * stage_no + 1], brecv.at[j, h, side, 2 * stage_no + 1],
                    toward(h, stage_no, sign))

    def b_close(j, stage_no):
        buf = rb2 if stage_no == 0 else rb4
        for h in (0, 1):
            bx[j, h, 0, stage_no, 1].wait_recv()
            bx[j, h, 1, stage_no, 1].wait_recv()
            part = piece(j, h, stage_no, 0, (0, 512))
            part[...] = part[...] + (buf[j, h, 0] + buf[j, h, 1])

    def b1(j):
        n = NA + j
        need(n, 0)
        core[n].wait_recv()

        def one(q, _):
            total = jnp.concatenate(
                [cr[n, 2 * q] + grad(n, 0, 2 * q), cr[n, 2 * q + 1] + grad(n, 0, 2 * q + 1)], axis=1)
            hi, lo = split(total)
            cols = pl.ds(pl.multiple_of(q * 256, 256), 256)
            pb[j, :, :, :, cols] = dot3(bth[...], btl[...], hi, lo).reshape(4, 4, 32, 256)
            return 0

        lax.fori_loop(0, 4, one, 0)
        b_first(j, 0)

    def b3(j):
        b_close(j, 0)
        b_first(j, 1)

    def b5(j):
        b_close(j, 1)

        def one(k, _):
            to = (z + k) % NZ
            cols = pl.ds(pl.multiple_of(to * LANE, LANE), LANE)
            pltpu.make_async_remote_copy(
                src_ref=pb.at[j, y, x, :, cols], dst_ref=qr.at[j, k - 1],
                send_sem=qsend.at[j], recv_sem=qrecv.at[j],
                device_id=(to * 2 + c, t), device_id_type=MESH).start()
            return 0

        lax.fori_loop(1, NZ, one, 0)

    def b6(j):
        wait_bytes(qr.at[j], qrecv.at[j])
        cols = pl.ds(pl.multiple_of(z * LANE, LANE), LANE)
        n = NA + j
        fin[:, n * LANE:(n + 1) * LANE] = pb[j, y, x, :, cols] + jnp.sum(qr[j], axis=0)

    def a2(j):
        a_send(j, 2)

    def a3(j):
        a_send(j, 3)

    def a4(j):
        a_send(j, 4)

    def b2(j):
        b_second(j, 0)

    def b4(j):
        b_second(j, 1)

    first_tiles = (0, 1, 4)
    for j in first_tiles:
        cast(j)
    small[0].wait()
    b = bbuf[...]
    hi, lo = split(b)
    bh[...] = hi
    bl[...] = lo
    hi, lo = split(b.T)
    bth[...] = hi
    btl[...] = lo
    pl.semaphore_wait(barrier, 30)
    for j in first_tiles:
        exchange(j)
    order = (
        (a1, 0), (a1, 1), (stage, 5), (b1, 0), (stage, 6), (stage, 2), (stage, 3),
        (a2, 0), (a2, 1), (b1, 1), (b2, 0), (a3, 0), (a3, 1), (b1, 2), (a4, 0), (b2, 1), (a4, 1),
        (b3, 0), (a1, 2), (a1, 3), (b4, 0), (a5, 0), (b2, 2), (a5, 1), (b5, 0), (a2, 2), (b3, 1), (a2, 3),
        (b4, 1), (a3, 2), (b3, 2), (a3, 3), (b5, 1), (b4, 2), (a4, 2), (b5, 2), (a4, 3),
        (a6, 0), (a6, 1), (b6, 0), (b6, 1), (a5, 2), (b6, 2), (a5, 3), (a6, 2), (a6, 3),
    )
    for step, j in order:
        step(j)

    acc = jnp.zeros((8, LANE), F32)
    for r in range(4):
        for j in range(7):
            v = fin[8 * r:8 * r + 8, LANE * j:LANE * (j + 1)]
            acc = acc + v * v

    def spread(buf, n, dev):
        def one(k, _):
            pltpu.make_async_remote_copy(
                src_ref=buf.at[15], dst_ref=buf.at[k - 1],
                send_sem=nsend.at[n], recv_sem=nrecv.at[n],
                device_id=dev(k), device_id_type=MESH).start()
            return 0

        lax.fori_loop(1, 16, one, 0)

    ssq1[15] = acc
    spread(ssq1, 0, lambda k: ((d + k) % 16, t))
    for cp in pending:
        cp.wait_send()
    pending.clear()
    for j in range(NA):
        wait_bytes(ar.at[j], asend.at[j])
    for j in range(NB):
        wait_bytes(qr.at[j], qsend.at[j])
    small[1].wait()
    small[2].wait()
    small[3].wait()
    wait_bytes(ssq1.at[0:15], nrecv.at[0])
    ssq2[15] = jnp.sum(ssq1[...], axis=0)
    spread(ssq2, 1, lambda k: (d, (t + k) % 16))
    wait_bytes(ssq1.at[0:15], nsend.at[0])
    wait_bytes(ssq2.at[0:15], nrecv.at[1])
    squares = jnp.sum(jnp.sum(ssq2[...], axis=0), axis=0, keepdims=True)
    squares = jnp.sum(squares, axis=1, keepdims=True)
    limit = 0.25 * (R * FFW) ** 0.5
    factor = jnp.minimum(jnp.float32(1.0), limit / (jnp.sqrt(squares) + 1e-06))

    clipped = factor * fin[...]
    new_first = 0.9 * m1[...] + 0.1 * clipped
    new_second = 0.95 * m2[...] + 0.05 * clipped * clipped
    m1[...] = new_first
    m2[...] = new_second
    dirs[y, x] = new_first / (1.0 - 0.9**STEP) / (jnp.sqrt(new_second / (1.0 - 0.95**STEP)) + 1e-08)

    span = ((0, 512), (512, 384))
    cut = (((0, 256), (256, 256)), ((512, 256), (768, 128)))
    dx = {}

    def rows_of(h, ring, k, cols):
        lane = pl.ds(*cols)
        if ring == 0:
            if h == 0:
                return dirs.at[y, (x + k + 4) % 4, :, lane]
            return dirs.at[(y + k + 4) % 4, x, :, lane]
        if h == 0:
            return dirs.at[(y + k + 4) % 4, :, :, lane]
        return dirs.at[:, (x + k + 4) % 4, :, lane]

    def d_send(h, ring, hop):
        for side, sign in ((0, 1), (1, -1)):
            if hop == 0:
                ref = rows_of(h, ring, 0, span[h])
            else:
                dx[h, ring, 0, side].wait_recv()
                ref = rows_of(h, ring, -sign, cut[h][side])
            n = 2 * ring + hop
            dx[h, ring, hop, side] = remote(
                ref, ref, dsend.at[h, n, side], drecv.at[h, n, side], toward(h, ring, sign))

    def d_wait(h, ring):
        dx[h, ring, 1, 0].wait_recv()
        dx[h, ring, 1, 1].wait_recv()

    d_send(0, 0, 0)
    d_send(1, 0, 0)
    outs = [
        pltpu.make_async_copy(m1, out_first_ref, lsem.at[1]),
        pltpu.make_async_copy(m2, out_second_ref, lsem.at[2]),
    ]
    for cp in outs:
        cp.start()
    d_send(0, 0, 1)
    d_send(1, 0, 1)
    d_wait(0, 0)
    d_send(0, 1, 0)
    d_wait(1, 0)
    d_send(1, 1, 0)
    d_send(0, 1, 1)
    d_send(1, 1, 1)
    wait_bytes(ssq2.at[0:15], nsend.at[1])
    for h in (0, 1):
        d_wait(h, 1)
        for n, (lo_col, width) in enumerate(cut[h]):
            cols = slice(lo_col, lo_col + width)
            hi, lo = split(dirs[:, :, :, cols].reshape(R, width))
            wbuf[:, cols] = wbuf[:, cols] - 0.5 * dot3(bh[...], bl[...], hi, lo)
            cp = pltpu.make_async_copy(wbuf.at[:, cols], out_ref.at[:, cols], lsem.at[3 + 2 * h + n])
            cp.start()
            outs.append(cp)
    for cp in pending:
        cp.wait_send()
    for cp in outs:
        cp.wait()


def body(grads, basis, weight, first_moment, second_moment):
    dma = pltpu.SemaphoreType.DMA
    vmem = pltpu.VMEM
    return pl.pallas_call(
        kernel,
        out_shape=(
            jax.ShapeDtypeStruct((ROWS, OWN), F32),
            jax.ShapeDtypeStruct((32, OWN), F32),
            jax.ShapeDtypeStruct((32, OWN), F32),
        ),
        in_specs=[pl.BlockSpec(memory_space=pl.ANY)] * 5,
        out_specs=[pl.BlockSpec(memory_space=pl.ANY)] * 3,
        scratch_shapes=[
            vmem((2, 2, NZ, ROWS, 256), BF16),
            vmem((2, NZ, ROWS, NB * LANE), BF16),
            vmem((NA + NB, NZ, ROWS, LANE), F32),
            vmem((NA + NB, NZ, ROWS, LANE), F32),
            vmem((NA, 2, 4, ROWS, LANE), F32),
            vmem((NB, 4, 4, 32, 1024), F32),
            vmem((NB, 2, 2, 4, 32, 256), F32),
            vmem((NB, 2, 2, 4, 32, 512), F32),
            vmem((NB, 2, 2, 32, 256), F32),
            vmem((NB, 2, 2, 32, 512), F32),
            vmem((NB, NZ - 1, 32, LANE), F32),
            vmem((NA, 16, 32, LANE), F32),
            vmem((NA, 15, 32, LANE), F32),
            vmem((32, OWN), F32),
            vmem((16, 8, LANE), F32),
            vmem((16, 8, LANE), F32),
            vmem((4, 4, 32, OWN), F32),
            vmem((ROWS, OWN), F32),
            vmem((32, OWN), F32),
            vmem((32, OWN), F32),
            vmem((ROWS, R), F32),
            vmem((R, ROWS), BF16),
            vmem((R, ROWS), BF16),
            vmem((ROWS, R), BF16),
            vmem((ROWS, R), BF16),
            dma((3, 2)),
            dma((7,)),
            dma((NA + NB,)), dma((NA + NB,)),
            dma((NA, 2, 4)), dma((NA, 2, 4)),
            dma((NA,)), dma((NA,)),
            dma((NB, 2, 2, 4)), dma((NB, 2, 2, 4)),
            dma((NB,)), dma((NB,)),
            dma((2,)), dma((2,)),
            dma((2, 4, 2)), dma((2, 4, 2)),
        ],
        compiler_params=pltpu.CompilerParams(
            collective_id=0, has_side_effects=True, vmem_limit_bytes=62 * 2**20),
        name="galore_step",
    )(grads[0], basis, weight, first_moment, second_moment)


def solution(mesh):
    in_specs = (
        P("dp", "tensor", None),
        P("tensor", None),
        P("tensor", "dp"),
        P("tensor", "dp"),
        P("tensor", "dp"),
    )
    out_specs = (P("tensor", "dp"), P("tensor", "dp"), P("tensor", "dp"))
    return jax.shard_map(body, mesh=mesh, in_specs=in_specs, out_specs=out_specs, check_vma=False)
```

```python
import jax
import jax.numpy as jnp
from jax import lax
from jax.experimental import pallas as pl
from jax.experimental.pallas import tpu as pltpu
from jax.sharding import PartitionSpec as P

FFW = 14336
R = 512
STEP = 10
OWN = 896
LANE = 128
ROWS = 256
NZ = 8
NA = 4
NB = 3
MESH = pl.DeviceIdType.MESH
F32 = jnp.float32
BF16 = jnp.bfloat16


def split(x):
    hi = x.astype(BF16)
    return hi, (x - hi.astype(F32)).astype(BF16)


def dot3(ah, al, bh, bl):
    def mm(a, b):
        return jnp.dot(a, b, preferred_element_type=F32)

    return mm(ah, bh) + (mm(ah, bl) + mm(al, bh))


def kernel(
    g_ref, basis_ref, first_ref, second_ref,
    out_ref, clipped_ref,
    ga, gb, cs, cr, zr, pb, rb1, rb2, rb3, rb4, qr, qz, pa, ah, hs, ar,
    fin, ssq1, ssq2, dirs, m1, m2, bbuf, bth, btl,
    gsem, lsem, fsend, frecv, csend, crecv, zsend, zrecv, asend, arecv,
    bsend, brecv, qsend, qrecv, hsend, hrecv, rsend, rrecv, nsend, nrecv, dsend, drecv,
):
    d = lax.axis_index("dp")
    t = lax.axis_index("tensor")
    z, c = d // 2, d % 2
    y, x = t // 4, t % 4

    def at_z(k):
        return (((z + k + NZ) % NZ) * 2 + c, t)

    def at_x(k):
        return (d, y * 4 + (x + k + 4) % 4)

    def at_y(k):
        return (d, ((y + k + 4) % 4) * 4 + x)

    partner = (z * 2 + 1 - c, t)

    def gload(group, which, start):
        core = c if which == 0 else 1 - c
        if group < 2:
            buf, lo, width = ga.at[which, group], 256 * group, 256
        else:
            buf, lo, width = gb.at[which], NA * LANE, NB * LANE
        sem = gsem.at[group, which]
        if not start:
            pltpu.make_async_copy(buf, buf, sem).wait()
            return

        def one(k, _):
            col = pl.multiple_of(OWN * (2 * ((z + 4 + k) % NZ) + core) + lo, LANE)
            pltpu.make_async_copy(g_ref.at[:, pl.ds(col, width)], buf.at[k], sem).start()
            return 0

        lax.fori_loop(0, NZ, one, 0)

    small = [
        pltpu.make_async_copy(basis_ref, bbuf, lsem.at[0]),
        pltpu.make_async_copy(first_ref, m1, lsem.at[1]),
        pltpu.make_async_copy(second_ref, m2, lsem.at[2]),
    ]
    gload(0, 1, True)
    gload(2, 1, True)
    gload(0, 0, True)
    small[0].start()
    gload(2, 0, True)
    gload(1, 1, True)
    gload(1, 0, True)
    for cp in small[1:]:
        cp.start()

    barrier = pltpu.get_barrier_semaphore()

    for to in (at_z(1), at_z(-1), at_x(1), at_x(-1), at_y(1), at_y(-1), partner):
        pl.semaphore_signal(barrier, 1, device_id=to, device_id_type=MESH)

    pending = []

    def remote(src, dst, ssem, rsem, dev):
        cp = pltpu.make_async_remote_copy(
            src_ref=src, dst_ref=dst, send_sem=ssem, recv_sem=rsem,
            device_id=dev, device_id_type=MESH,
        )
        cp.start()
        pending.append(cp)
        return cp

    loaded = set()

    def grad(j, which, k):
        if j < NA:
            return ga[which, j // 2, k, :, (j % 2) * LANE:(j % 2 + 1) * LANE].astype(F32)
        return gb[which, k, :, (j - NA) * LANE:(j - NA + 1) * LANE].astype(F32)

    def need(j, which):
        group = j // 2 if j < NA else 2
        if (group, which) not in loaded:
            loaded.add((group, which))
            gload(group, which, False)

    core = {}
    far = {}

    def cast(j, lo, hi):
        need(j, 1)

        def one(k, _):
            cs[j, k] = grad(j, 1, k)
            return 0

        lax.fori_loop(lo, hi, one, 0)

    def send_far(j):
        far[j] = remote(cs.at[j, 0], cr.at[j, 0], fsend.at[j], frecv.at[j], partner)

    def send_rest(j):
        core[j] = remote(cs.at[j, 1:NZ], cr.at[j, 1:NZ], csend.at[j], crecv.at[j], partner)

    def stage(j):
        cast(j, 0, NZ)
        if j < NA:
            send_far(j)
            send_rest(j)
        else:
            core[j] = remote(cs.at[j], cr.at[j], csend.at[j], crecv.at[j], partner)

    az = {}
    waited = set()

    def once(table, *keys):
        for key in keys:
            if (id(table), key) not in waited:
                waited.add((id(table), key))
                table[key].wait_recv()

    def a_send(j, s):
        for side, sign in ((0, 1), (1, -1)):
            dest = (4 + sign * (5 - s)) % NZ
            rows = pl.ds(0, ROWS)
            if s == 1:
                rows = pl.ds(128 * side, 128)
            elif s == 2:
                az[j, side, 1].wait_recv()
                half = pl.ds(128 * side, 128)
                cr[j, dest, half] = cr[j, dest, half] + zr[j, side, 0, 0:128]
            else:
                az[j, side, s - 1].wait_recv()
                cr[j, dest] = cr[j, dest] + zr[j, side, s - 2]
            to = zr.at[j, side, 0, 0:128] if s == 1 else zr.at[j, side, s - 1]
            az[j, side, s] = remote(
                cr.at[j, dest, rows], to,
                zsend.at[j, side, s - 1], zrecv.at[j, side, s - 1], at_z(sign))

    def a0(j):
        need(j, 0)
        far[j].wait_recv()
        cr[j, 0] = cr[j, 0] + grad(j, 0, 0)
        a_send(j, 1)

    def a1(j):
        core[j].wait_recv()

        def one(k, _):
            cr[j, k] = cr[j, k] + grad(j, 0, k)
            return 0

        lax.fori_loop(1, NZ, one, 0)

    def spread(src, dst, ssem, rsem, peers):
        for k, to in enumerate(peers):
            pltpu.make_async_remote_copy(
                src_ref=src(k + 1), dst_ref=dst.at[k], send_sem=ssem, recv_sem=rsem,
                device_id=to, device_id_type=MESH).start()

    def line(over_x):
        return [at_x(k) if over_x else at_y(k) for k in (1, 2, 3)]

    def a5(j):
        once(az, (j, 0, 4), (j, 1, 4))
        total = cr[j, 4] + zr[j, 0, 3] + zr[j, 1, 3]
        hi, lo = split(total)
        pa[j] = dot3(bth[...], btl[...], hi, lo).reshape(4, 4, 32, LANE)
        if j >= 2:
            spread(
                lambda k: pa.at[j, (t + k) % 16 // 4, (t + k) % 4], ar.at[j],
                asend.at[j], arecv.at[j], [(d, (t + k) % 16) for k in range(1, 16)])
        elif j == 0:
            spread(lambda k: pa.at[j, :, (x + k) % 4], ah.at[j], hsend.at[j], hrecv.at[j], line(True))
        else:
            spread(lambda k: pa.at[j, (y + k) % 4], ah.at[j], hsend.at[j], hrecv.at[j], line(False))

    def a7(j):
        wait_bytes(ah.at[j], hrecv.at[j])
        if j == 0:
            hs[j] = pa[j, :, x] + (ah[j, 0] + ah[j, 1] + ah[j, 2])
            spread(lambda k: hs.at[j, (y + k) % 4], ar.at[j], asend.at[j], arecv.at[j], line(False))
        else:
            hs[j] = pa[j, y] + (ah[j, 0] + ah[j, 1] + ah[j, 2])
            spread(lambda k: hs.at[j, (x + k) % 4], ar.at[j], asend.at[j], arecv.at[j], line(True))

    def wait_bytes(ref, sem):
        pltpu.make_async_copy(ref, ref, sem).wait()

    def a6(j):
        cols = slice(j * LANE, (j + 1) * LANE)
        if j >= 2:
            wait_bytes(ar.at[j], arecv.at[j])
            fin[:, cols] = pa[j, y, x] + jnp.sum(ar[j], axis=0)
        else:
            wait_bytes(ar.at[j, 0:3], arecv.at[j])
            fin[:, cols] = hs[j, y if j == 0 else x] + (ar[j, 0] + ar[j, 1] + ar[j, 2])

    bx = {}

    def piece(j, h, stage_no, k, cols):
        lane = pl.ds(512 * h + cols[0], cols[1])
        if stage_no == 0:
            if h == 0:
                return pb.at[j, :, (x + k + 4) % 4, :, lane]
            return pb.at[j, (y + k + 4) % 4, :, :, lane]
        if h == 0:
            return pb.at[j, (y + k + 4) % 4, x, :, lane]
        return pb.at[j, y, (x + k + 4) % 4, :, lane]

    def toward(h, stage_no, k):
        return at_x(k) if (h + stage_no) % 2 == 0 else at_y(k)

    def b_first(j, stage_no):
        buf = rb1 if stage_no == 0 else rb3
        for h in (0, 1):
            for side, sign in ((0, 1), (1, -1)):
                bx[j, h, side, stage_no, 0] = remote(
                    piece(j, h, stage_no, 2, (256 * side, 256)), buf.at[j, h, side],
                    bsend.at[j, h, side, 2 * stage_no], brecv.at[j, h, side, 2 * stage_no],
                    toward(h, stage_no, sign))

    def b_second(j, stage_no):
        got, buf = (rb1, rb2) if stage_no == 0 else (rb3, rb4)
        for h in (0, 1):
            for side, sign in ((0, 1), (1, -1)):
                bx[j, h, side, stage_no, 0].wait_recv()
                part = piece(j, h, stage_no, sign, (256 * side, 256))
                part[...] = part[...] + got[j, h, side]
                bx[j, h, side, stage_no, 1] = remote(
                    piece(j, h, stage_no, sign, (0, 512)), buf.at[j, h, side],
                    bsend.at[j, h, side, 2 * stage_no + 1], brecv.at[j, h, side, 2 * stage_no + 1],
                    toward(h, stage_no, sign))

    def b_close(j, stage_no):
        buf = rb2 if stage_no == 0 else rb4
        for h in (0, 1):
            once(bx, (j, h, 0, stage_no, 1), (j, h, 1, stage_no, 1))
            part = piece(j, h, stage_no, 0, (0, 512))
            part[...] = part[...] + (buf[j, h, 0] + buf[j, h, 1])

    def b1(j):
        n = NA + j
        need(n, 0)
        core[n].wait_recv()

        def one(q, _):
            total = jnp.concatenate(
                [cr[n, 2 * q] + grad(n, 0, 2 * q), cr[n, 2 * q + 1] + grad(n, 0, 2 * q + 1)], axis=1)
            hi, lo = split(total)
            cols = pl.ds(pl.multiple_of(q * 256, 256), 256)
            pb[j, :, :, :, cols] = dot3(bth[...], btl[...], hi, lo).reshape(4, 4, 32, 256)
            return 0

        lax.fori_loop(0, 4, one, 0)
        b_first(j, 0)

    def b3(j):
        b_close(j, 0)
        b_first(j, 1)

    rx = {}

    def r_send(j, s):
        for side, sign in ((0, 1), (1, -1)):
            dest = (4 + sign * (5 - s)) % NZ
            col = slice(LANE * dest, LANE * (dest + 1))
            rows = slice(0, 32)
            if s <= 2:
                half = slice(16 * side, 16 * side + 16)
            if s == 1:
                rows = half
            else:
                rx[j, side, s - 1].wait_recv()
                if s == 2:
                    pb[j, y, x, half, col] = pb[j, y, x, half, col] + qz[side, 0, 0:16]
                else:
                    pb[j, y, x, :, col] = pb[j, y, x, :, col] + qz[side, s - 2]
            to = qz.at[side, 0, 0:16] if s == 1 else qz.at[side, s - 1]
            rx[j, side, s] = remote(
                pb.at[j, y, x, rows, col], to,
                rsend.at[side, s - 1], rrecv.at[side, s - 1], at_z(sign))

    def b5(j):
        b_close(j, 1)
        if j == 0:
            r_send(j, 1)
            return

        def block(k):
            col = LANE * ((4 + k) % NZ)
            return pb.at[j, y, x, :, col:col + LANE]

        spread(block, qr.at[j], qsend.at[j], qrecv.at[j], [at_z(k) for k in range(1, NZ)])

    def b6(j):
        n = NA + j
        own = pb[j, y, x, :, 4 * LANE:5 * LANE]
        if j == 0:
            rx[j, 0, 4].wait_recv()
            rx[j, 1, 4].wait_recv()
            fin[:, n * LANE:(n + 1) * LANE] = own + (qz[0, 3] + qz[1, 3])
        else:
            wait_bytes(qr.at[j], qrecv.at[j])
            fin[:, n * LANE:(n + 1) * LANE] = own + jnp.sum(qr[j], axis=0)

    def meet(_):
        once(az, (0, 0, 4), (0, 1, 4))
        once(bx, *[(0, h, side, 1, 1) for h in (0, 1) for side in (0, 1)])

    def r2(j):
        r_send(j, 2)

    def r3(j):
        r_send(j, 3)

    def r4(j):
        r_send(j, 4)

    def a2(j):
        a_send(j, 2)

    def a3(j):
        a_send(j, 3)

    def a4(j):
        a_send(j, 4)

    def b2(j):
        b_second(j, 0)

    def b4(j):
        b_second(j, 1)

    cast(0, 0, 1)
    cast(1, 0, 1)
    pl.semaphore_wait(barrier, 7)
    send_far(0)
    send_far(1)
    stage(4)
    for j in (0, 1):
        cast(j, 1, NZ)
        send_rest(j)
    small[0].wait()
    hi, lo = split(bbuf[...].T)
    bth[...] = hi
    btl[...] = lo
    def flush(_):
        for cp in pending:
            cp.wait_send()
        pending.clear()
        small[1].wait()
        small[2].wait()

    order = (
        (a0, 0), (a0, 1), (stage, 5), (stage, 2), (stage, 3), (b1, 0), (a1, 0), (a2, 0), (stage, 6), (a1, 1),
        (a2, 1), (b1, 1), (a0, 2), (a0, 3), (a1, 2), (b2, 0), (a3, 0), (a1, 3), (b1, 2), (a3, 1), (a2, 2),
        (a4, 0), (b3, 0), (b2, 1), (a4, 1), (a2, 3), (b4, 0), (b2, 2), (a3, 2), (b3, 1), (a5, 0), (meet, 0),
        (b5, 0), (a5, 1), (a3, 3), (b3, 2), (a4, 2), (r2, 0), (b4, 1), (a4, 3), (a7, 0), (a7, 1), (b4, 2),
        (b5, 1), (a5, 2), (r3, 0), (a6, 1), (a6, 0), (b5, 2), (a5, 3), (r4, 0), (a6, 2), (b6, 1), (b6, 0),
        (flush, 0), (a6, 3), (b6, 2),
    )
    for step, j in order:
        step(j)

    acc = jnp.zeros((8, LANE), F32)
    for r in range(4):
        for j in range(7):
            v = fin[8 * r:8 * r + 8, LANE * j:LANE * (j + 1)]
            acc = acc + v * v

    ssq1[15] = acc
    spread(lambda k: ssq1.at[15], ssq1, nsend.at[0], nrecv.at[0], [((d + k) % 16, t) for k in range(1, 16)])
    wait_bytes(ssq1.at[0:15], nrecv.at[0])
    ssq2[15] = jnp.sum(ssq1[...], axis=0)
    spread(lambda k: ssq2.at[15], ssq2, nsend.at[1], nrecv.at[1], [(d, (t + k) % 16) for k in range(1, 16)])
    wait_bytes(ssq2.at[0:15], nrecv.at[1])
    squares = jnp.sum(jnp.sum(ssq2[...], axis=0), axis=0, keepdims=True)
    squares = jnp.sum(squares, axis=1, keepdims=True)
    limit = 0.25 * (R * FFW) ** 0.5
    factor = jnp.minimum(jnp.float32(1.0), limit / (jnp.sqrt(squares) + 1e-06))

    clipped = factor * fin[...]
    new_first = 0.9 * m1[...] + 0.1 * clipped
    new_second = 0.95 * m2[...] + 0.05 * clipped * clipped
    dirs[y, x] = new_first / (1.0 - 0.9**STEP) / (jnp.sqrt(new_second / (1.0 - 0.95**STEP)) + 1e-08)

    dx = {}
    firsts = (0, -1, 1, 2)
    sides = ((0, 1), (1, -1))

    def d_send(h, ring, hop, n, side, first, second, part):
        yo, xo = (second, first) if h == 0 else (first, second)
        ref = dirs.at[(y + yo + 4) % 4, (x + xo + 4) % 4, pl.ds(16 * h + part[0], part[1])]
        dx[h, ring, hop, n, side] = remote(
            ref, ref, dsend.at[h, ring, hop, n, side], drecv.at[h, ring, hop, n, side],
            toward(h, ring, sides[side][1]))

    def d_forward(n):
        for h in (0, 1):
            for side, sign in sides:
                dx[h, 1, 0, n, side].wait_recv()
                d_send(h, 1, 1, n, side, firsts[n], -sign, (8 * side, 8))

    for ring in (0, 1):
        for h in (0, 1):
            for side, _ in sides:
                d_send(h, ring, 0, 0, side, 0, 0, (0, 16))
    m1[...] = clipped
    out = pltpu.make_async_copy(m1, clipped_ref, lsem.at[1])
    out.start()
    for side, sign in sides:
        for h in (0, 1):
            dx[h, 0, 0, 0, side].wait_recv()
            d_send(h, 0, 1, 0, side, -sign, 0, (8 * side, 8))
            for other, _ in sides:
                d_send(h, 1, 0, 1 + side, other, -sign, 0, (0, 16))
    for j in (0, 1):
        wait_bytes(ah.at[j], hsend.at[j])
        wait_bytes(ar.at[j, 0:3], asend.at[j])
    for j in (2, 3):
        wait_bytes(ar.at[j], asend.at[j])
    for j in (1, 2):
        wait_bytes(qr.at[j], qsend.at[j])
    wait_bytes(ssq1.at[0:15], nsend.at[0])
    d_forward(0)
    for h in (0, 1):
        for side, _ in sides:
            dx[h, 0, 1, 0, side].wait_recv()
        for other, _ in sides:
            d_send(h, 1, 0, 3, other, 2, 0, (0, 16))
    for n in (1, 2, 3):
        d_forward(n)
    wait_bytes(ssq2.at[0:15], nsend.at[1])
    for n in range(4):
        for h in (0, 1):
            for side, _ in sides:
                dx[h, 1, 1, n, side].wait_recv()
    last = pltpu.make_async_copy(dirs, out_ref, lsem.at[2])
    last.start()
    for cp in pending:
        cp.wait_send()
    out.wait()
    last.wait()


def finish(
    dir_ref, clipped_ref, basis_ref, weight_ref, first_ref, second_ref,
    out_ref, out_first_ref, out_second_ref,
    dbuf, bbuf, wbuf, clipped, m1, m2, sem, osem,
):
    parts = ((0, 256), (256, 256), (512, 256), (768, 128))
    loads = [
        pltpu.make_async_copy(basis_ref, bbuf, sem.at[0]),
        pltpu.make_async_copy(clipped_ref, clipped, sem.at[1]),
        pltpu.make_async_copy(first_ref, m1, sem.at[2]),
        pltpu.make_async_copy(second_ref, m2, sem.at[3]),
    ]
    for n, (lo, width) in enumerate(parts):
        cols = pl.ds(lo, width)
        loads.append(pltpu.make_async_copy(dir_ref.at[:, cols], dbuf.at[:, cols], sem.at[4 + n]))
    for n, (lo, width) in enumerate(parts):
        cols = pl.ds(lo, width)
        loads.append(pltpu.make_async_copy(weight_ref.at[:, cols], wbuf.at[:, cols], sem.at[8 + n]))
    for cp in loads:
        cp.start()
    loads[0].wait()
    bh, bl = split(bbuf[...])
    for cp in loads[1:4]:
        cp.wait()
    m1[...] = 0.9 * m1[...] + 0.1 * clipped[...]
    m2[...] = 0.95 * m2[...] + 0.05 * clipped[...] * clipped[...]
    outs = [
        pltpu.make_async_copy(m1, out_first_ref, osem.at[0]),
        pltpu.make_async_copy(m2, out_second_ref, osem.at[1]),
    ]
    for cp in outs:
        cp.start()
    for n, (lo, width) in enumerate(parts):
        cols = slice(lo, lo + width)
        loads[4 + n].wait()
        loads[8 + n].wait()
        dh, dl = split(dbuf[:, cols])
        wbuf[:, cols] = wbuf[:, cols] - 0.5 * dot3(bh, bl, dh, dl)
        cp = pltpu.make_async_copy(wbuf.at[:, cols], out_ref.at[:, cols], osem.at[2 + n])
        cp.start()
        outs.append(cp)
    for cp in outs:
        cp.wait()


def body(grads, basis, weight, first_moment, second_moment):
    dma = pltpu.SemaphoreType.DMA
    vmem = pltpu.VMEM
    any_ = pl.BlockSpec(memory_space=pl.ANY)
    direction, clipped = pl.pallas_call(
        kernel,
        out_shape=(
            jax.ShapeDtypeStruct((4, 4, 32, OWN), F32),
            jax.ShapeDtypeStruct((32, OWN), F32),
        ),
        in_specs=[any_] * 4,
        out_specs=[any_] * 2,
        scratch_shapes=[
            vmem((2, 2, NZ, ROWS, 256), BF16),
            vmem((2, NZ, ROWS, NB * LANE), BF16),
            vmem((NA + NB, NZ, ROWS, LANE), F32),
            vmem((NA + NB, NZ, ROWS, LANE), F32),
            vmem((NA, 2, 4, ROWS, LANE), F32),
            vmem((NB, 4, 4, 32, 1024), F32),
            vmem((NB, 2, 2, 4, 32, 256), F32),
            vmem((NB, 2, 2, 4, 32, 512), F32),
            vmem((NB, 2, 2, 32, 256), F32),
            vmem((NB, 2, 2, 32, 512), F32),
            vmem((NB, NZ - 1, 32, LANE), F32),
            vmem((2, 4, 32, LANE), F32),
            vmem((NA, 4, 4, 32, LANE), F32),
            vmem((2, 3, 4, 32, LANE), F32),
            vmem((2, 4, 32, LANE), F32),
            vmem((NA, 15, 32, LANE), F32),
            vmem((32, OWN), F32),
            vmem((16, 8, LANE), F32),
            vmem((16, 8, LANE), F32),
            vmem((4, 4, 32, OWN), F32),
            vmem((32, OWN), F32),
            vmem((32, OWN), F32),
            vmem((ROWS, R), F32),
            vmem((R, ROWS), BF16),
            vmem((R, ROWS), BF16),
            dma((3, 2)),
            dma((3,)),
            dma((NA,)), dma((NA,)),
            dma((NA + NB,)), dma((NA + NB,)),
            dma((NA, 2, 4)), dma((NA, 2, 4)),
            dma((NA,)), dma((NA,)),
            dma((NB, 2, 2, 4)), dma((NB, 2, 2, 4)),
            dma((NB,)), dma((NB,)),
            dma((2,)), dma((2,)),
            dma((2, 4)), dma((2, 4)),
            dma((2,)), dma((2,)),
            dma((2, 2, 2, 4, 2)), dma((2, 2, 2, 4, 2)),
        ],
        compiler_params=pltpu.CompilerParams(
            collective_id=0, has_side_effects=True, vmem_limit_bytes=62 * 2**20),
        name="galore_step",
    )(grads[0], basis, first_moment, second_moment)
    return pl.pallas_call(
        finish,
        out_shape=(
            jax.ShapeDtypeStruct((ROWS, OWN), F32),
            jax.ShapeDtypeStruct((32, OWN), F32),
            jax.ShapeDtypeStruct((32, OWN), F32),
        ),
        in_specs=[any_] * 6,
        out_specs=[any_] * 3,
        scratch_shapes=[
            vmem((R, OWN), F32), vmem((ROWS, R), F32), vmem((ROWS, OWN), F32),
            vmem((32, OWN), F32), vmem((32, OWN), F32), vmem((32, OWN), F32),
            dma((12,)), dma((6,)),
        ],
        compiler_params=pltpu.CompilerParams(vmem_limit_bytes=62 * 2**20),
        name="galore_update",
    )(direction.reshape(R, OWN), clipped, basis, weight, first_moment, second_moment)


def solution(mesh):
    in_specs = (
        P("dp", "tensor", None),
        P("tensor", None),
        P("tensor", "dp"),
        P("tensor", "dp"),
        P("tensor", "dp"),
    )
    out_specs = (P("tensor", "dp"), P("tensor", "dp"), P("tensor", "dp"))
    return jax.shard_map(body, mesh=mesh, in_specs=in_specs, out_specs=out_specs, check_vma=False)
```

```python
import jax
import jax.numpy as jnp
from jax import lax
from jax.experimental import pallas as pl
from jax.experimental.pallas import tpu as pltpu
from jax.sharding import PartitionSpec as P

FFW = 14336
R = 512
STEP = 10
OWN = 896
LANE = 128
ROWS = 256
NZ = 8
NA = 4
NB = 3
MESH = pl.DeviceIdType.MESH
F32 = jnp.float32
BF16 = jnp.bfloat16


def split(x):
    hi = x.astype(BF16)
    return hi, (x - hi.astype(F32)).astype(BF16)


def dot3(ah, al, bh, bl):
    def mm(a, b):
        return jnp.dot(a, b, preferred_element_type=F32)

    return mm(ah, bh) + (mm(ah, bl) + mm(al, bh))


def kernel(
    g_ref, basis_ref, first_ref, second_ref,
    out_ref, clipped_ref,
    ga, gb, cs, cr, zr, pb, rb1, rb2, rb3, rb4, qr, qz, pa, ah, hs, ar,
    fin, ssq1, ssq2, dirs, delta, m1, m2, bbuf, bth, btl, bh, bl,
    gsem, lsem, fsend, frecv, csend, crecv, zsend, zrecv, asend, arecv,
    bsend, brecv, qsend, qrecv, hsend, hrecv, rsend, rrecv, nsend, nrecv, dsend, drecv,
):
    d = lax.axis_index("dp")
    t = lax.axis_index("tensor")
    z, c = d // 2, d % 2
    y, x = t // 4, t % 4

    def at_z(k):
        return (((z + k + NZ) % NZ) * 2 + c, t)

    def at_x(k):
        return (d, y * 4 + (x + k + 4) % 4)

    def at_y(k):
        return (d, ((y + k + 4) % 4) * 4 + x)

    partner = (z * 2 + 1 - c, t)

    barrier = pltpu.get_barrier_semaphore()

    for to in (at_z(1), at_z(-1), at_x(1), at_x(-1), at_y(1), at_y(-1), partner):
        pl.semaphore_signal(barrier, 1, device_id=to, device_id_type=MESH)

    def gload(group, which, start):
        core = c if which == 0 else 1 - c
        first, last = (1, NZ) if group == 0 else (0, 1) if group == 3 else (0, NZ)
        if group != 2:
            buf, lo, width = ga.at[which, group % 3], 256 * (group % 3), 256
        else:
            buf, lo, width = gb.at[which], NA * LANE, NB * LANE
        sem = gsem.at[group, which]
        if not start:
            part = buf.at[first:last]
            pltpu.make_async_copy(part, part, sem).wait()
            return

        def one(k, _):
            col = pl.multiple_of(OWN * (2 * ((z + 4 + k) % NZ) + core) + lo, LANE)
            pltpu.make_async_copy(g_ref.at[:, pl.ds(col, width)], buf.at[k], sem).start()
            return 0

        lax.fori_loop(first, last, one, 0)

    small = [
        pltpu.make_async_copy(basis_ref, bbuf, lsem.at[0]),
        pltpu.make_async_copy(first_ref, m1, lsem.at[1]),
        pltpu.make_async_copy(second_ref, m2, lsem.at[2]),
    ]
    gload(3, 1, True)
    gload(3, 0, True)
    gload(2, 1, True)
    gload(0, 1, True)
    small[0].start()
    gload(0, 0, True)
    gload(2, 0, True)
    gload(1, 1, True)
    gload(1, 0, True)
    for cp in small[1:]:
        cp.start()

    pending = []

    def remote(src, dst, ssem, rsem, dev):
        cp = pltpu.make_async_remote_copy(
            src_ref=src, dst_ref=dst, send_sem=ssem, recv_sem=rsem,
            device_id=dev, device_id_type=MESH,
        )
        cp.start()
        pending.append(cp)
        return cp

    loaded = set()

    def grad(j, which, k):
        if j < NA:
            return ga[which, j // 2, k, :, (j % 2) * LANE:(j % 2 + 1) * LANE].astype(F32)
        return gb[which, k, :, (j - NA) * LANE:(j - NA + 1) * LANE].astype(F32)

    def need(j, which, far_only=False):
        group = j // 2 if j < NA else 2
        for part in (3,) if far_only and group == 0 else (3, 0) if group == 0 else (group,):
            if (part, which) not in loaded:
                loaded.add((part, which))
                gload(part, which, False)

    core = {}
    far = {}

    def cast(j, lo, hi):
        need(j, 1, hi == 1)

        def one(k, _):
            cs[j, k] = grad(j, 1, k)
            return 0

        lax.fori_loop(lo, hi, one, 0)

    def send_far(j):
        far[j] = remote(cs.at[j, 0], cr.at[j, 0], fsend.at[j], frecv.at[j], partner)

    def send_rest(j):
        core[j] = remote(cs.at[j, 1:NZ], cr.at[j, 1:NZ], csend.at[j], crecv.at[j], partner)

    def stage(j):
        cast(j, 0, NZ)
        if j < NA:
            send_far(j)
            send_rest(j)
        else:
            core[j] = remote(cs.at[j], cr.at[j], csend.at[j], crecv.at[j], partner)

    az = {}
    waited = set()

    def once(table, *keys):
        for key in keys:
            if (id(table), key) not in waited:
                waited.add((id(table), key))
                table[key].wait_recv()

    def a_send(j, s):
        for side, sign in ((0, 1), (1, -1)):
            dest = (4 + sign * (5 - s)) % NZ
            rows = pl.ds(0, ROWS)
            if s == 1:
                rows = pl.ds(128 * side, 128)
            elif s == 2:
                az[j, side, 1].wait_recv()
                half = pl.ds(128 * side, 128)
                cr[j, dest, half] = cr[j, dest, half] + zr[j, side, 0, 0:128]
            else:
                az[j, side, s - 1].wait_recv()
                cr[j, dest] = cr[j, dest] + zr[j, side, s - 2]
            to = zr.at[j, side, 0, 0:128] if s == 1 else zr.at[j, side, s - 1]
            az[j, side, s] = remote(
                cr.at[j, dest, rows], to,
                zsend.at[j, side, s - 1], zrecv.at[j, side, s - 1], at_z(sign))

    def a0(j):
        need(j, 0, True)
        far[j].wait_recv()
        cr[j, 0] = cr[j, 0] + grad(j, 0, 0)
        a_send(j, 1)

    def a1(j):
        need(j, 0)
        core[j].wait_recv()

        def one(k, _):
            cr[j, k] = cr[j, k] + grad(j, 0, k)
            return 0

        lax.fori_loop(1, NZ, one, 0)

    def spread(src, dst, ssem, rsem, peers):
        for k, to in enumerate(peers):
            pltpu.make_async_remote_copy(
                src_ref=src(k + 1), dst_ref=dst.at[k], send_sem=ssem, recv_sem=rsem,
                device_id=to, device_id_type=MESH).start()

    def line(over_x):
        return [at_x(k) if over_x else at_y(k) for k in (1, 2, 3)]

    def a5(j):
        once(az, (j, 0, 4), (j, 1, 4))
        total = cr[j, 4] + zr[j, 0, 3] + zr[j, 1, 3]
        hi, lo = split(total)
        pa[j] = dot3(bth[...], btl[...], hi, lo).reshape(4, 4, 32, LANE)
        if j >= 2:
            spread(
                lambda k: pa.at[j, (t + k) % 16 // 4, (t + k) % 4], ar.at[j],
                asend.at[j], arecv.at[j], [(d, (t + k) % 16) for k in range(1, 16)])
        elif j == 0:
            spread(lambda k: pa.at[j, :, (x + k) % 4], ah.at[j], hsend.at[j], hrecv.at[j], line(True))
        else:
            spread(lambda k: pa.at[j, (y + k) % 4], ah.at[j], hsend.at[j], hrecv.at[j], line(False))

    def a7(j):
        wait_bytes(ah.at[j], hrecv.at[j])
        if j == 0:
            hs[j] = pa[j, :, x] + (ah[j, 0] + ah[j, 1] + ah[j, 2])
            spread(lambda k: hs.at[j, (y + k) % 4], ar.at[j], asend.at[j], arecv.at[j], line(False))
        else:
            hs[j] = pa[j, y] + (ah[j, 0] + ah[j, 1] + ah[j, 2])
            spread(lambda k: hs.at[j, (x + k) % 4], ar.at[j], asend.at[j], arecv.at[j], line(True))

    def wait_bytes(ref, sem):
        pltpu.make_async_copy(ref, ref, sem).wait()

    def a6(j):
        cols = slice(j * LANE, (j + 1) * LANE)
        if j >= 2:
            wait_bytes(ar.at[j], arecv.at[j])
            fin[:, cols] = pa[j, y, x] + jnp.sum(ar[j], axis=0)
        else:
            wait_bytes(ar.at[j, 0:3], arecv.at[j])
            fin[:, cols] = hs[j, y if j == 0 else x] + (ar[j, 0] + ar[j, 1] + ar[j, 2])

    bx = {}

    def piece(j, h, stage_no, k, cols):
        lane = pl.ds(512 * h + cols[0], cols[1])
        if stage_no == 0:
            if h == 0:
                return pb.at[j, :, (x + k + 4) % 4, :, lane]
            return pb.at[j, (y + k + 4) % 4, :, :, lane]
        if h == 0:
            return pb.at[j, (y + k + 4) % 4, x, :, lane]
        return pb.at[j, y, (x + k + 4) % 4, :, lane]

    def toward(h, stage_no, k):
        return at_x(k) if (h + stage_no) % 2 == 0 else at_y(k)

    def b_first(j, stage_no):
        buf = rb1 if stage_no == 0 else rb3
        for h in (0, 1):
            for side, sign in ((0, 1), (1, -1)):
                bx[j, h, side, stage_no, 0] = remote(
                    piece(j, h, stage_no, 2, (256 * side, 256)), buf.at[j, h, side],
                    bsend.at[j, h, side, 2 * stage_no], brecv.at[j, h, side, 2 * stage_no],
                    toward(h, stage_no, sign))

    def b_second(j, stage_no):
        got, buf = (rb1, rb2) if stage_no == 0 else (rb3, rb4)
        for h in (0, 1):
            for side, sign in ((0, 1), (1, -1)):
                bx[j, h, side, stage_no, 0].wait_recv()
                part = piece(j, h, stage_no, sign, (256 * side, 256))
                part[...] = part[...] + got[j, h, side]
                bx[j, h, side, stage_no, 1] = remote(
                    piece(j, h, stage_no, sign, (0, 512)), buf.at[j, h, side],
                    bsend.at[j, h, side, 2 * stage_no + 1], brecv.at[j, h, side, 2 * stage_no + 1],
                    toward(h, stage_no, sign))

    def b_close(j, stage_no):
        buf = rb2 if stage_no == 0 else rb4
        for h in (0, 1):
            once(bx, (j, h, 0, stage_no, 1), (j, h, 1, stage_no, 1))
            part = piece(j, h, stage_no, 0, (0, 512))
            part[...] = part[...] + (buf[j, h, 0] + buf[j, h, 1])

    def b1(j):
        n = NA + j
        need(n, 0)
        core[n].wait_recv()

        def one(q, _):
            total = jnp.concatenate(
                [cr[n, 2 * q] + grad(n, 0, 2 * q), cr[n, 2 * q + 1] + grad(n, 0, 2 * q + 1)], axis=1)
            hi, lo = split(total)
            cols = pl.ds(pl.multiple_of(q * 256, 256), 256)
            pb[j, :, :, :, cols] = dot3(bth[...], btl[...], hi, lo).reshape(4, 4, 32, 256)
            return 0

        lax.fori_loop(0, 4, one, 0)
        b_first(j, 0)

    def b3(j):
        b_close(j, 0)
        b_first(j, 1)

    rx = {}

    def r_send(j, s):
        for side, sign in ((0, 1), (1, -1)):
            dest = (4 + sign * (5 - s)) % NZ
            col = slice(LANE * dest, LANE * (dest + 1))
            rows = slice(0, 32)
            if s <= 2:
                half = slice(16 * side, 16 * side + 16)
            if s == 1:
                rows = half
            else:
                rx[j, side, s - 1].wait_recv()
                if s == 2:
                    pb[j, y, x, half, col] = pb[j, y, x, half, col] + qz[side, 0, 0:16]
                else:
                    pb[j, y, x, :, col] = pb[j, y, x, :, col] + qz[side, s - 2]
            to = qz.at[side, 0, 0:16] if s == 1 else qz.at[side, s - 1]
            rx[j, side, s] = remote(
                pb.at[j, y, x, rows, col], to,
                rsend.at[side, s - 1], rrecv.at[side, s - 1], at_z(sign))

    def b5(j):
        b_close(j, 1)
        if j == 0:
            r_send(j, 1)
            return

        def block(k):
            col = LANE * ((4 + k) % NZ)
            return pb.at[j, y, x, :, col:col + LANE]

        spread(block, qr.at[j], qsend.at[j], qrecv.at[j], [at_z(k) for k in range(1, NZ)])

    def b6(j):
        n = NA + j
        own = pb[j, y, x, :, 4 * LANE:5 * LANE]
        if j == 0:
            rx[j, 0, 4].wait_recv()
            rx[j, 1, 4].wait_recv()
            fin[:, n * LANE:(n + 1) * LANE] = own + (qz[0, 3] + qz[1, 3])
        else:
            wait_bytes(qr.at[j], qrecv.at[j])
            fin[:, n * LANE:(n + 1) * LANE] = own + jnp.sum(qr[j], axis=0)

    def meet(_):
        once(az, (0, 0, 4), (0, 1, 4))
        once(bx, *[(0, h, side, 1, 1) for h in (0, 1) for side in (0, 1)])

    def r2(j):
        r_send(j, 2)

    def r3(j):
        r_send(j, 3)

    def r4(j):
        r_send(j, 4)

    def a2(j):
        a_send(j, 2)

    def a3(j):
        a_send(j, 3)

    def a4(j):
        a_send(j, 4)

    def b2(j):
        b_second(j, 0)

    def b4(j):
        b_second(j, 1)

    firsts = (0, -1, 1, 2)
    sides = ((0, 1), (1, -1))

    def gather(buf):
        dx = {}

        def send(h, ring, hop, n, side, first, second, part):
            yo, xo = (second, first) if h == 0 else (first, second)
            ref = buf.at[(y + yo + 4) % 4, (x + xo + 4) % 4, pl.ds(16 * h + part[0], part[1])]
            dx[h, ring, hop, n, side] = remote(
                ref, ref, dsend.at[h, ring, hop, n, side], drecv.at[h, ring, hop, n, side],
                toward(h, ring, sides[side][1]))

        def forward(n):
            for h in (0, 1):
                for side, sign in sides:
                    dx[h, 1, 0, n, side].wait_recv()
                    send(h, 1, 1, n, side, firsts[n], -sign, (8 * side, 8))

        def g0():
            for ring in (0, 1):
                for h in (0, 1):
                    for side, _ in sides:
                        send(h, ring, 0, 0, side, 0, 0, (0, 16))

        def g1():
            for side, sign in sides:
                for h in (0, 1):
                    dx[h, 0, 0, 0, side].wait_recv()
                    send(h, 0, 1, 0, side, -sign, 0, (8 * side, 8))
                    for other, _ in sides:
                        send(h, 1, 0, 1 + side, other, -sign, 0, (0, 16))

        def g2():
            forward(0)

        def g3():
            for h in (0, 1):
                for side, _ in sides:
                    dx[h, 0, 1, 0, side].wait_recv()
                for other, _ in sides:
                    send(h, 1, 0, 3, other, 2, 0, (0, 16))

        def g4():
            forward(1)
            forward(2)

        def g5():
            forward(3)

        def close():
            for n in range(4):
                for h in (0, 1):
                    for side, _ in sides:
                        dx[h, 1, 1, n, side].wait_recv()

        return g0, g1, g2, g3, g4, g5, close

    cast(0, 0, 1)
    cast(1, 0, 1)
    pl.semaphore_wait(barrier, 7)
    send_far(0)
    send_far(1)
    stage(4)

    def rest(j):
        cast(j, 1, NZ)
        send_rest(j)

    def prep(_):
        small[0].wait()
        hi, lo = split(bbuf[...].T)
        bth[...] = hi
        btl[...] = lo

    def flush(_):
        for cp in pending:
            cp.wait_send()
        pending.clear()
        for cp in small[1:]:
            cp.wait()
        hi, lo = split(bbuf[...])
        bh[...] = hi
        bl[...] = lo

    order = (
        (rest, 0), (prep, 0), (a0, 0), (a0, 1), (stage, 2), (stage, 6), (rest, 1), (b1, 0), (a0, 2), (a1, 0),
        (a2, 0), (stage, 3), (stage, 5), (a1, 2), (a2, 2), (b1, 2), (a1, 1), (a2, 1), (a0, 3), (a1, 3),
        (a3, 0), (b2, 0), (b1, 1), (a3, 2), (b2, 2), (a3, 1), (a2, 3), (b3, 0), (a4, 0), (b2, 1), (a4, 1),
        (b3, 2), (a3, 3), (b4, 0), (a4, 2), (b3, 1), (b4, 2), (a5, 1), (a5, 0), (meet, 0), (b5, 0), (a4, 3),
        (b4, 1), (r2, 0), (b5, 2), (a5, 2), (a5, 3), (r3, 0), (b5, 1), (a7, 0), (a7, 1), (r4, 0), (b6, 2),
        (a6, 2), (b6, 0), (a6, 0), (a6, 1), (flush, 0), (a6, 3), (b6, 1),
    )
    for step, j in order:
        step(j)

    acc = jnp.zeros((8, LANE), F32)
    for r in range(4):
        for j in range(7):
            v = fin[8 * r:8 * r + 8, LANE * j:LANE * (j + 1)]
            acc = acc + v * v

    ssq1[15] = acc
    spread(lambda k: ssq1.at[15], ssq1, nsend.at[0], nrecv.at[0], [((d + k) % 16, t) for k in range(1, 16)])
    wait_bytes(ssq1.at[0:15], nrecv.at[0])
    ssq2[15] = jnp.sum(ssq1[...], axis=0)
    spread(lambda k: ssq2.at[15], ssq2, nsend.at[1], nrecv.at[1], [(d, (t + k) % 16) for k in range(1, 16)])
    wait_bytes(ssq2.at[0:15], nrecv.at[1])
    squares = jnp.sum(jnp.sum(ssq2[...], axis=0), axis=0, keepdims=True)
    squares = jnp.sum(squares, axis=1, keepdims=True)
    limit = 0.25 * (R * FFW) ** 0.5
    factor = jnp.minimum(jnp.float32(1.0), limit / (jnp.sqrt(squares) + 1e-06))

    clipped = factor * fin[...]
    new_first = 0.9 * m1[...] + 0.1 * clipped
    new_second = 0.95 * m2[...] + 0.05 * clipped * clipped
    dirs[y, x] = new_first / (1.0 - 0.9**STEP) / (jnp.sqrt(new_second / (1.0 - 0.95**STEP)) + 1e-08)
    d0, d1, d2, d3, d4, d5, direction_here = gather(dirs)
    d0()
    fin[...] = clipped
    outs = [pltpu.make_async_copy(fin, clipped_ref, lsem.at[0])]
    outs[0].start()

    d1()
    d2()
    d3()
    d4()
    for j in (0, 1):
        wait_bytes(ah.at[j], hsend.at[j])
        wait_bytes(ar.at[j, 0:3], asend.at[j])
    for j in (2, 3):
        wait_bytes(ar.at[j], asend.at[j])
    for j in (1, 2):
        wait_bytes(qr.at[j], qsend.at[j])
    wait_bytes(ssq1.at[0:15], nsend.at[0])
    wait_bytes(ssq2.at[0:15], nsend.at[1])
    d5()
    direction_here()
    for n, (lo_col, width) in enumerate(((0, 256), (256, 256), (512, 256), (768, 128))):
        cols = slice(lo_col, lo_col + width)
        hi, lo = split(dirs[:, :, :, cols].reshape(R, width))
        delta[:, cols] = dot3(bh[...], bl[...], hi, lo)
        outs.append(pltpu.make_async_copy(delta.at[:, cols], out_ref.at[:, cols], lsem.at[1 + n]))
        outs[-1].start()
    for cp in pending:
        cp.wait_send()
    for cp in outs:
        cp.wait()


def finish(
    delta_ref, clipped_ref, weight_ref, first_ref, second_ref,
    out_ref, out_first_ref, out_second_ref,
    dbuf, wbuf, clipped, m1, m2, sem, osem,
):
    loads = []
    for n in range(4):
        rows = pl.ds(64 * n, 64)
        loads.append(pltpu.make_async_copy(weight_ref.at[rows], wbuf.at[rows], sem.at[2 * n]))
        loads.append(pltpu.make_async_copy(delta_ref.at[rows], dbuf.at[rows], sem.at[2 * n + 1]))
    loads.append(pltpu.make_async_copy(clipped_ref, clipped, sem.at[8]))
    loads.append(pltpu.make_async_copy(first_ref, m1, sem.at[9]))
    loads.append(pltpu.make_async_copy(second_ref, m2, sem.at[10]))
    for cp in loads:
        cp.start()
    outs = []
    for n in range(4):
        rows = slice(64 * n, 64 * n + 64)
        loads[2 * n].wait()
        loads[2 * n + 1].wait()
        wbuf[rows] = wbuf[rows] - 0.5 * dbuf[rows]
        outs.append(pltpu.make_async_copy(wbuf.at[rows], out_ref.at[rows], osem.at[n]))
        outs[-1].start()
    for cp in loads[8:]:
        cp.wait()
    m1[...] = 0.9 * m1[...] + 0.1 * clipped[...]
    m2[...] = 0.95 * m2[...] + 0.05 * clipped[...] * clipped[...]
    for n, (src, dst) in enumerate(((m1, out_first_ref), (m2, out_second_ref))):
        outs.append(pltpu.make_async_copy(src, dst, osem.at[4 + n]))
        outs[-1].start()
    for cp in outs:
        cp.wait()


def body(grads, basis, weight, first_moment, second_moment):
    dma = pltpu.SemaphoreType.DMA
    vmem = pltpu.VMEM
    any_ = pl.BlockSpec(memory_space=pl.ANY)
    delta, clipped = pl.pallas_call(
        kernel,
        out_shape=(
            jax.ShapeDtypeStruct((ROWS, OWN), F32),
            jax.ShapeDtypeStruct((32, OWN), F32),
        ),
        in_specs=[any_] * 4,
        out_specs=[any_] * 2,
        scratch_shapes=[
            vmem((2, 2, NZ, ROWS, 256), BF16),
            vmem((2, NZ, ROWS, NB * LANE), BF16),
            vmem((NA + NB, NZ, ROWS, LANE), F32),
            vmem((NA + NB, NZ, ROWS, LANE), F32),
            vmem((NA, 2, 4, ROWS, LANE), F32),
            vmem((NB, 4, 4, 32, 1024), F32),
            vmem((NB, 2, 2, 4, 32, 256), F32),
            vmem((NB, 2, 2, 4, 32, 512), F32),
            vmem((NB, 2, 2, 32, 256), F32),
            vmem((NB, 2, 2, 32, 512), F32),
            vmem((NB, NZ - 1, 32, LANE), F32),
            vmem((2, 4, 32, LANE), F32),
            vmem((NA, 4, 4, 32, LANE), F32),
            vmem((2, 3, 4, 32, LANE), F32),
            vmem((2, 4, 32, LANE), F32),
            vmem((NA, 15, 32, LANE), F32),
            vmem((32, OWN), F32),
            vmem((16, 8, LANE), F32),
            vmem((16, 8, LANE), F32),
            vmem((4, 4, 32, OWN), F32),
            vmem((ROWS, OWN), F32),
            vmem((32, OWN), F32),
            vmem((32, OWN), F32),
            vmem((ROWS, R), F32),
            vmem((R, ROWS), BF16),
            vmem((R, ROWS), BF16),
            vmem((ROWS, R), BF16),
            vmem((ROWS, R), BF16),
            dma((4, 2)),
            dma((5,)),
            dma((NA,)), dma((NA,)),
            dma((NA + NB,)), dma((NA + NB,)),
            dma((NA, 2, 4)), dma((NA, 2, 4)),
            dma((NA,)), dma((NA,)),
            dma((NB, 2, 2, 4)), dma((NB, 2, 2, 4)),
            dma((NB,)), dma((NB,)),
            dma((2,)), dma((2,)),
            dma((2, 4)), dma((2, 4)),
            dma((2,)), dma((2,)),
            dma((2, 2, 2, 4, 2)), dma((2, 2, 2, 4, 2)),
        ],
        compiler_params=pltpu.CompilerParams(
            collective_id=0, has_side_effects=True, vmem_limit_bytes=62 * 2**20),
        name="galore_step",
    )(grads[0], basis, first_moment, second_moment)
    return pl.pallas_call(
        finish,
        out_shape=(
            jax.ShapeDtypeStruct((ROWS, OWN), F32),
            jax.ShapeDtypeStruct((32, OWN), F32),
            jax.ShapeDtypeStruct((32, OWN), F32),
        ),
        in_specs=[any_] * 5,
        out_specs=[any_] * 3,
        scratch_shapes=[
            vmem((ROWS, OWN), F32), vmem((ROWS, OWN), F32),
            vmem((32, OWN), F32), vmem((32, OWN), F32), vmem((32, OWN), F32),
            dma((11,)), dma((6,)),
        ],
        compiler_params=pltpu.CompilerParams(vmem_limit_bytes=62 * 2**20),
        name="galore_update",
    )(delta, clipped, weight, first_moment, second_moment)


def solution(mesh):
    in_specs = (
        P("dp", "tensor", None),
        P("tensor", None),
        P("tensor", "dp"),
        P("tensor", "dp"),
        P("tensor", "dp"),
    )
    out_specs = (P("tensor", "dp"), P("tensor", "dp"), P("tensor", "dp"))
    return jax.shard_map(body, mesh=mesh, in_specs=in_specs, out_specs=out_specs, check_vma=False)
```

```python
import jax
import jax.numpy as jnp
from jax import lax
from jax.experimental import pallas as pl
from jax.experimental.pallas import tpu as pltpu
from jax.sharding import PartitionSpec as P

FFW = 14336
R = 512
STEP = 10
OWN = 896
LANE = 128
ROWS = 256
NZ = 8
NA = 4
NB = 3
MESH = pl.DeviceIdType.MESH
F32 = jnp.float32
BF16 = jnp.bfloat16


def split(x):
    hi = x.astype(BF16)
    return hi, (x - hi.astype(F32)).astype(BF16)


def dot3(ah, al, bh, bl):
    def mm(a, b):
        return jnp.dot(a, b, preferred_element_type=F32)

    return mm(ah, bh) + (mm(ah, bl) + mm(al, bh))


def kernel(
    g_ref, basis_ref, first_ref, second_ref,
    out_ref, clipped_ref,
    ga, gb, cs, cr, zr, pb, rb1, rb2, rb3, rb4, qr, qz, pa, ah, hs, ar,
    fin, ssq1, ssq2, dirs, delta, m1, m2, bbuf, bth, btl, bh, bl,
    gsem, lsem, fsend, frecv, csend, crecv, zsend, zrecv, asend, arecv,
    bsend, brecv, qsend, qrecv, hsend, hrecv, rsend, rrecv, nsend, nrecv, dsend, drecv,
):
    d = lax.axis_index("dp")
    t = lax.axis_index("tensor")
    z, c = d // 2, d % 2
    y, x = t // 4, t % 4

    def at_z(k):
        return (((z + k + NZ) % NZ) * 2 + c, t)

    def at_x(k):
        return (d, y * 4 + (x + k + 4) % 4)

    def at_y(k):
        return (d, ((y + k + 4) % 4) * 4 + x)

    partner = (z * 2 + 1 - c, t)

    barrier = pltpu.get_barrier_semaphore()

    for to in (at_z(1), at_z(-1), at_x(1), at_x(-1), at_y(1), at_y(-1), partner):
        pl.semaphore_signal(barrier, 1, device_id=to, device_id_type=MESH)

    def gload(group, which, start):
        core = c if which == 0 else 1 - c
        first, last = (1, NZ) if group == 0 else (0, 1) if group == 3 else (0, NZ)
        if group != 2:
            buf, lo, width = ga.at[which, group % 3], 256 * (group % 3), 256
        else:
            buf, lo, width = gb.at[which], NA * LANE, NB * LANE
        sem = gsem.at[group, which]
        if not start:
            part = buf.at[first:last]
            pltpu.make_async_copy(part, part, sem).wait()
            return

        def one(k, _):
            col = pl.multiple_of(OWN * (2 * ((z + 4 + k) % NZ) + core) + lo, LANE)
            pltpu.make_async_copy(g_ref.at[:, pl.ds(col, width)], buf.at[k], sem).start()
            return 0

        lax.fori_loop(first, last, one, 0)

    small = [
        pltpu.make_async_copy(basis_ref, bbuf, lsem.at[0]),
        pltpu.make_async_copy(first_ref, m1, lsem.at[1]),
        pltpu.make_async_copy(second_ref, m2, lsem.at[2]),
    ]
    gload(3, 1, True)
    gload(3, 0, True)
    gload(2, 1, True)
    gload(0, 1, True)
    small[0].start()
    gload(0, 0, True)
    gload(2, 0, True)
    gload(1, 1, True)
    gload(1, 0, True)
    for cp in small[1:]:
        cp.start()

    pending = []

    def remote(src, dst, ssem, rsem, dev):
        cp = pltpu.make_async_remote_copy(
            src_ref=src, dst_ref=dst, send_sem=ssem, recv_sem=rsem,
            device_id=dev, device_id_type=MESH,
        )
        cp.start()
        pending.append(cp)
        return cp

    loaded = set()

    def grad(j, which, k):
        if j < NA:
            return ga[which, j // 2, k, :, (j % 2) * LANE:(j % 2 + 1) * LANE].astype(F32)
        return gb[which, k, :, (j - NA) * LANE:(j - NA + 1) * LANE].astype(F32)

    def need(j, which, far_only=False):
        group = j // 2 if j < NA else 2
        for part in (3,) if far_only and group == 0 else (3, 0) if group == 0 else (group,):
            if (part, which) not in loaded:
                loaded.add((part, which))
                gload(part, which, False)

    core = {}
    far = {}

    def cast(j, lo, hi):
        need(j, 1, hi == 1)

        def one(k, _):
            cs[j, k] = grad(j, 1, k)
            return 0

        lax.fori_loop(lo, hi, one, 0)

    def send_far(j):
        far[j] = remote(cs.at[j, 0], cr.at[j, 0], fsend.at[j], frecv.at[j], partner)

    def send_rest(j):
        core[j] = remote(cs.at[j, 1:NZ], cr.at[j, 1:NZ], csend.at[j], crecv.at[j], partner)

    def stage(j):
        cast(j, 0, NZ)
        if j < NA:
            send_far(j)
            send_rest(j)
        else:
            core[j] = remote(cs.at[j], cr.at[j], csend.at[j], crecv.at[j], partner)

    az = {}
    waited = set()

    def once(table, *keys):
        for key in keys:
            if (id(table), key) not in waited:
                waited.add((id(table), key))
                table[key].wait_recv()

    def a_send(j, s):
        for side, sign in ((0, 1), (1, -1)):
            dest = (4 + sign * (5 - s)) % NZ
            rows = pl.ds(0, ROWS)
            if s == 1:
                rows = pl.ds(128 * side, 128)
            elif s == 2:
                az[j, side, 1].wait_recv()
                half = pl.ds(128 * side, 128)
                cr[j, dest, half] = cr[j, dest, half] + zr[j, side, 0, 0:128]
            else:
                az[j, side, s - 1].wait_recv()
                cr[j, dest] = cr[j, dest] + zr[j, side, s - 2]
            to = zr.at[j, side, 0, 0:128] if s == 1 else zr.at[j, side, s - 1]
            az[j, side, s] = remote(
                cr.at[j, dest, rows], to,
                zsend.at[j, side, s - 1], zrecv.at[j, side, s - 1], at_z(sign))

    def a0(j):
        need(j, 0, True)
        far[j].wait_recv()
        cr[j, 0] = cr[j, 0] + grad(j, 0, 0)
        a_send(j, 1)

    def a1(j):
        need(j, 0)
        core[j].wait_recv()

        def one(k, _):
            cr[j, k] = cr[j, k] + grad(j, 0, k)
            return 0

        lax.fori_loop(1, NZ, one, 0)

    def spread(src, dst, ssem, rsem, peers):
        for k, to in enumerate(peers):
            pltpu.make_async_remote_copy(
                src_ref=src(k + 1), dst_ref=dst.at[k], send_sem=ssem, recv_sem=rsem,
                device_id=to, device_id_type=MESH).start()

    def line(over_x):
        return [at_x(k) if over_x else at_y(k) for k in (1, 2, 3)]

    def a5(j):
        once(az, (j, 0, 4), (j, 1, 4))
        total = cr[j, 4] + zr[j, 0, 3] + zr[j, 1, 3]
        hi, lo = split(total)
        pa[j] = dot3(bth[...], btl[...], hi, lo).reshape(4, 4, 32, LANE)
        if j >= 2:
            spread(
                lambda k: pa.at[j, (t + k) % 16 // 4, (t + k) % 4], ar.at[j],
                asend.at[j], arecv.at[j], [(d, (t + k) % 16) for k in range(1, 16)])
        elif j == 0:
            spread(lambda k: pa.at[j, :, (x + k) % 4], ah.at[j], hsend.at[j], hrecv.at[j], line(True))
        else:
            spread(lambda k: pa.at[j, (y + k) % 4], ah.at[j], hsend.at[j], hrecv.at[j], line(False))

    def a7(j):
        wait_bytes(ah.at[j], hrecv.at[j])
        if j == 0:
            hs[j] = pa[j, :, x] + (ah[j, 0] + ah[j, 1] + ah[j, 2])
            spread(lambda k: hs.at[j, (y + k) % 4], ar.at[j], asend.at[j], arecv.at[j], line(False))
        else:
            hs[j] = pa[j, y] + (ah[j, 0] + ah[j, 1] + ah[j, 2])
            spread(lambda k: hs.at[j, (x + k) % 4], ar.at[j], asend.at[j], arecv.at[j], line(True))

    def wait_bytes(ref, sem):
        pltpu.make_async_copy(ref, ref, sem).wait()

    def a6(j):
        cols = slice(j * LANE, (j + 1) * LANE)
        if j >= 2:
            wait_bytes(ar.at[j], arecv.at[j])
            fin[:, cols] = pa[j, y, x] + jnp.sum(ar[j], axis=0)
        else:
            wait_bytes(ar.at[j, 0:3], arecv.at[j])
            fin[:, cols] = hs[j, y if j == 0 else x] + (ar[j, 0] + ar[j, 1] + ar[j, 2])

    bx = {}

    def piece(j, h, stage_no, k, cols):
        lane = pl.ds(512 * h + cols[0], cols[1])
        if stage_no == 0:
            if h == 0:
                return pb.at[j, :, (x + k + 4) % 4, :, lane]
            return pb.at[j, (y + k + 4) % 4, :, :, lane]
        if h == 0:
            return pb.at[j, (y + k + 4) % 4, x, :, lane]
        return pb.at[j, y, (x + k + 4) % 4, :, lane]

    def toward(h, stage_no, k):
        return at_x(k) if (h + stage_no) % 2 == 0 else at_y(k)

    def b_first(j, stage_no):
        buf = rb1 if stage_no == 0 else rb3
        for h in (0, 1):
            for side, sign in ((0, 1), (1, -1)):
                bx[j, h, side, stage_no, 0] = remote(
                    piece(j, h, stage_no, 2, (256 * side, 256)), buf.at[j, h, side],
                    bsend.at[j, h, side, 2 * stage_no], brecv.at[j, h, side, 2 * stage_no],
                    toward(h, stage_no, sign))

    def b_second(j, stage_no):
        got, buf = (rb1, rb2) if stage_no == 0 else (rb3, rb4)
        for h in (0, 1):
            for side, sign in ((0, 1), (1, -1)):
                bx[j, h, side, stage_no, 0].wait_recv()
                part = piece(j, h, stage_no, sign, (256 * side, 256))
                part[...] = part[...] + got[j, h, side]
                bx[j, h, side, stage_no, 1] = remote(
                    piece(j, h, stage_no, sign, (0, 512)), buf.at[j, h, side],
                    bsend.at[j, h, side, 2 * stage_no + 1], brecv.at[j, h, side, 2 * stage_no + 1],
                    toward(h, stage_no, sign))

    def b_close(j, stage_no):
        buf = rb2 if stage_no == 0 else rb4
        for h in (0, 1):
            once(bx, (j, h, 0, stage_no, 1), (j, h, 1, stage_no, 1))
            part = piece(j, h, stage_no, 0, (0, 512))
            part[...] = part[...] + (buf[j, h, 0] + buf[j, h, 1])

    def b1(j):
        n = NA + j
        need(n, 0)
        core[n].wait_recv()

        def one(q, _):
            total = jnp.concatenate(
                [cr[n, 2 * q] + grad(n, 0, 2 * q), cr[n, 2 * q + 1] + grad(n, 0, 2 * q + 1)], axis=1)
            hi, lo = split(total)
            cols = pl.ds(pl.multiple_of(q * 256, 256), 256)
            pb[j, :, :, :, cols] = dot3(bth[...], btl[...], hi, lo).reshape(4, 4, 32, 256)
            return 0

        lax.fori_loop(0, 4, one, 0)
        b_first(j, 0)

    def b3(j):
        b_close(j, 0)
        b_first(j, 1)

    rx = {}

    def r_send(j, s):
        for side, sign in ((0, 1), (1, -1)):
            dest = (4 + sign * (5 - s)) % NZ
            col = slice(LANE * dest, LANE * (dest + 1))
            rows = slice(0, 32)
            if s <= 2:
                half = slice(16 * side, 16 * side + 16)
            if s == 1:
                rows = half
            else:
                rx[j, side, s - 1].wait_recv()
                if s == 2:
                    pb[j, y, x, half, col] = pb[j, y, x, half, col] + qz[side, 0, 0:16]
                else:
                    pb[j, y, x, :, col] = pb[j, y, x, :, col] + qz[side, s - 2]
            to = qz.at[side, 0, 0:16] if s == 1 else qz.at[side, s - 1]
            rx[j, side, s] = remote(
                pb.at[j, y, x, rows, col], to,
                rsend.at[side, s - 1], rrecv.at[side, s - 1], at_z(sign))

    def b5(j):
        b_close(j, 1)
        if j == 0:
            r_send(j, 1)
            return

        def block(k):
            col = LANE * ((4 + k) % NZ)
            return pb.at[j, y, x, :, col:col + LANE]

        spread(block, qr.at[j], qsend.at[j], qrecv.at[j], [at_z(k) for k in range(1, NZ)])

    def b6(j):
        n = NA + j
        own = pb[j, y, x, :, 4 * LANE:5 * LANE]
        if j == 0:
            rx[j, 0, 4].wait_recv()
            rx[j, 1, 4].wait_recv()
            fin[:, n * LANE:(n + 1) * LANE] = own + (qz[0, 3] + qz[1, 3])
        else:
            wait_bytes(qr.at[j], qrecv.at[j])
            fin[:, n * LANE:(n + 1) * LANE] = own + jnp.sum(qr[j], axis=0)

    def meet(_):
        once(az, (0, 0, 4), (0, 1, 4))
        once(bx, *[(0, h, side, 1, 1) for h in (0, 1) for side in (0, 1)])

    def r2(j):
        r_send(j, 2)

    def r3(j):
        r_send(j, 3)

    def r4(j):
        r_send(j, 4)

    def a2(j):
        a_send(j, 2)

    def a3(j):
        a_send(j, 3)

    def a4(j):
        a_send(j, 4)

    def b2(j):
        b_second(j, 0)

    def b4(j):
        b_second(j, 1)

    firsts = (0, -1, 1, 2)
    sides = ((0, 1), (1, -1))

    def gather(buf):
        dx = {}

        def send(h, ring, hop, n, side, first, second, part):
            yo, xo = (second, first) if h == 0 else (first, second)
            ref = buf.at[(y + yo + 4) % 4, (x + xo + 4) % 4, pl.ds(16 * h + part[0], part[1])]
            dx[h, ring, hop, n, side] = remote(
                ref, ref, dsend.at[h, ring, hop, n, side], drecv.at[h, ring, hop, n, side],
                toward(h, ring, sides[side][1]))

        def own():
            for ring in (0, 1):
                for h in (0, 1):
                    for side, _ in sides:
                        send(h, ring, 0, 0, side, 0, 0, (0, 16))

        def first_halves():
            for side, sign in sides:
                for h in (0, 1):
                    dx[h, 0, 0, 0, side].wait_recv()
                    send(h, 0, 1, 0, side, -sign, 0, (8 * side, 8))

        def second(n):
            for h in (0, 1):
                if n == 3:
                    for side, _ in sides:
                        dx[h, 0, 1, 0, side].wait_recv()
                for side, _ in sides:
                    send(h, 1, 0, n, side, firsts[n], 0, (0, 16))

        def second_halves(n):
            for h in (0, 1):
                for side, sign in sides:
                    dx[h, 1, 0, n, side].wait_recv()
                    send(h, 1, 1, n, side, firsts[n], -sign, (8 * side, 8))

        def close():
            for n in range(4):
                for h in (0, 1):
                    for side, _ in sides:
                        dx[h, 1, 1, n, side].wait_recv()

        return own, first_halves, second, second_halves, close

    cast(0, 0, 1)
    cast(1, 0, 1)
    pl.semaphore_wait(barrier, 7)
    send_far(0)
    send_far(1)
    stage(4)

    def rest(j):
        cast(j, 1, NZ)
        send_rest(j)

    def prep(_):
        small[0].wait()
        hi, lo = split(bbuf[...].T)
        bth[...] = hi
        btl[...] = lo

    def flush(_):
        for cp in pending:
            cp.wait_send()
        pending.clear()
        for cp in small[1:]:
            cp.wait()
        hi, lo = split(bbuf[...])
        bh[...] = hi
        bl[...] = lo

    order = (
        (rest, 1), (stage, 5), (a0, 1), (a0, 0), (rest, 0), (stage, 3), (prep, 0), (b1, 0), (a1, 1), (a2, 1),
        (stage, 6), (b1, 1), (a1, 0), (a2, 0), (stage, 2), (a1, 3), (b2, 0), (a0, 2), (a0, 3), (b1, 2),
        (a1, 2), (a3, 0), (a2, 2), (a3, 1), (a2, 3), (b3, 0), (b2, 1), (b2, 2), (a3, 2), (b4, 0), (a4, 0),
        (b3, 1), (a4, 2), (a3, 3), (b3, 2), (meet, 0), (b5, 0), (a4, 1), (b4, 1), (a5, 2), (b4, 2), (a5, 0),
        (r2, 0), (a4, 3), (a5, 1), (r3, 0), (b5, 1), (b5, 2), (a6, 2), (a5, 3), (r4, 0), (a7, 0), (a7, 1),
        (b6, 1), (b6, 0), (a6, 1), (a6, 0), (flush, 0), (a6, 3), (b6, 2),
    )
    for step, j in order:
        step(j)

    acc = jnp.zeros((8, LANE), F32)
    for r in range(4):
        for j in range(7):
            v = fin[8 * r:8 * r + 8, LANE * j:LANE * (j + 1)]
            acc = acc + v * v

    ssq1[15] = acc
    spread(lambda k: ssq1.at[15], ssq1, nsend.at[0], nrecv.at[0], [((d + k) % 16, t) for k in range(1, 16)])
    wait_bytes(ssq1.at[0:15], nrecv.at[0])
    ssq2[15] = jnp.sum(ssq1[...], axis=0)
    spread(lambda k: ssq2.at[15], ssq2, nsend.at[1], nrecv.at[1], [(d, (t + k) % 16) for k in range(1, 16)])
    wait_bytes(ssq2.at[0:15], nrecv.at[1])
    squares = jnp.sum(jnp.sum(ssq2[...], axis=0), axis=0, keepdims=True)
    squares = jnp.sum(squares, axis=1, keepdims=True)
    limit = 0.25 * (R * FFW) ** 0.5
    factor = jnp.minimum(jnp.float32(1.0), limit / (jnp.sqrt(squares) + 1e-06))

    clipped = factor * fin[...]
    new_first = 0.9 * m1[...] + 0.1 * clipped
    new_second = 0.95 * m2[...] + 0.05 * clipped * clipped
    dirs[y, x] = new_first / (1.0 - 0.9**STEP) / (jnp.sqrt(new_second / (1.0 - 0.95**STEP)) + 1e-08)
    own, first_halves, second, second_halves, close = gather(dirs)
    own()
    fin[...] = clipped
    outs = [pltpu.make_async_copy(fin, clipped_ref, lsem.at[0])]
    outs[0].start()

    first_halves()
    for n in (1, 2, 3):
        second(n)
    for n in (0, 1, 2):
        second_halves(n)
    for j in (0, 1):
        wait_bytes(ah.at[j], hsend.at[j])
        wait_bytes(ar.at[j, 0:3], asend.at[j])
    for j in (2, 3):
        wait_bytes(ar.at[j], asend.at[j])
    for j in (1, 2):
        wait_bytes(qr.at[j], qsend.at[j])
    wait_bytes(ssq1.at[0:15], nsend.at[0])
    wait_bytes(ssq2.at[0:15], nsend.at[1])
    second_halves(3)
    close()
    for n, (lo_col, width) in enumerate(((0, 256), (256, 256), (512, 256), (768, 128))):
        cols = slice(lo_col, lo_col + width)
        hi, lo = split(dirs[:, :, :, cols].reshape(R, width))
        delta[:, cols] = dot3(bh[...], bl[...], hi, lo)
        outs.append(pltpu.make_async_copy(delta.at[:, cols], out_ref.at[:, cols], lsem.at[1 + n]))
        outs[-1].start()
    for cp in pending:
        cp.wait_send()
    for cp in outs:
        cp.wait()


def finish(
    delta_ref, clipped_ref, weight_ref, first_ref, second_ref,
    out_ref, out_first_ref, out_second_ref,
    dbuf, wbuf, clipped, m1, m2, sem, osem,
):
    loads = []
    for n in range(4):
        rows = pl.ds(64 * n, 64)
        loads.append(pltpu.make_async_copy(weight_ref.at[rows], wbuf.at[rows], sem.at[2 * n]))
        loads.append(pltpu.make_async_copy(delta_ref.at[rows], dbuf.at[rows], sem.at[2 * n + 1]))
    loads.append(pltpu.make_async_copy(clipped_ref, clipped, sem.at[8]))
    loads.append(pltpu.make_async_copy(first_ref, m1, sem.at[9]))
    loads.append(pltpu.make_async_copy(second_ref, m2, sem.at[10]))
    for cp in loads:
        cp.start()
    outs = []
    for n in range(4):
        rows = slice(64 * n, 64 * n + 64)
        loads[2 * n].wait()
        loads[2 * n + 1].wait()
        wbuf[rows] = wbuf[rows] - 0.5 * dbuf[rows]
        outs.append(pltpu.make_async_copy(wbuf.at[rows], out_ref.at[rows], osem.at[n]))
        outs[-1].start()
    for cp in loads[8:]:
        cp.wait()
    m1[...] = 0.9 * m1[...] + 0.1 * clipped[...]
    m2[...] = 0.95 * m2[...] + 0.05 * clipped[...] * clipped[...]
    for n, (src, dst) in enumerate(((m1, out_first_ref), (m2, out_second_ref))):
        outs.append(pltpu.make_async_copy(src, dst, osem.at[4 + n]))
        outs[-1].start()
    for cp in outs:
        cp.wait()


def body(grads, basis, weight, first_moment, second_moment):
    dma = pltpu.SemaphoreType.DMA
    vmem = pltpu.VMEM
    any_ = pl.BlockSpec(memory_space=pl.ANY)
    delta, clipped = pl.pallas_call(
        kernel,
        out_shape=(
            jax.ShapeDtypeStruct((ROWS, OWN), F32),
            jax.ShapeDtypeStruct((32, OWN), F32),
        ),
        in_specs=[any_] * 4,
        out_specs=[any_] * 2,
        scratch_shapes=[
            vmem((2, 2, NZ, ROWS, 256), BF16),
            vmem((2, NZ, ROWS, NB * LANE), BF16),
            vmem((NA + NB, NZ, ROWS, LANE), F32),
            vmem((NA + NB, NZ, ROWS, LANE), F32),
            vmem((NA, 2, 4, ROWS, LANE), F32),
            vmem((NB, 4, 4, 32, 1024), F32),
            vmem((NB, 2, 2, 4, 32, 256), F32),
            vmem((NB, 2, 2, 4, 32, 512), F32),
            vmem((NB, 2, 2, 32, 256), F32),
            vmem((NB, 2, 2, 32, 512), F32),
            vmem((NB, NZ - 1, 32, LANE), F32),
            vmem((2, 4, 32, LANE), F32),
            vmem((NA, 4, 4, 32, LANE), F32),
            vmem((2, 3, 4, 32, LANE), F32),
            vmem((2, 4, 32, LANE), F32),
            vmem((NA, 15, 32, LANE), F32),
            vmem((32, OWN), F32),
            vmem((16, 8, LANE), F32),
            vmem((16, 8, LANE), F32),
            vmem((4, 4, 32, OWN), F32),
            vmem((ROWS, OWN), F32),
            vmem((32, OWN), F32),
            vmem((32, OWN), F32),
            vmem((ROWS, R), F32),
            vmem((R, ROWS), BF16),
            vmem((R, ROWS), BF16),
            vmem((ROWS, R), BF16),
            vmem((ROWS, R), BF16),
            dma((4, 2)),
            dma((5,)),
            dma((NA,)), dma((NA,)),
            dma((NA + NB,)), dma((NA + NB,)),
            dma((NA, 2, 4)), dma((NA, 2, 4)),
            dma((NA,)), dma((NA,)),
            dma((NB, 2, 2, 4)), dma((NB, 2, 2, 4)),
            dma((NB,)), dma((NB,)),
            dma((2,)), dma((2,)),
            dma((2, 4)), dma((2, 4)),
            dma((2,)), dma((2,)),
            dma((2, 2, 2, 4, 2)), dma((2, 2, 2, 4, 2)),
        ],
        compiler_params=pltpu.CompilerParams(
            collective_id=0, has_side_effects=True, vmem_limit_bytes=62 * 2**20),
        name="galore_step",
    )(grads[0], basis, first_moment, second_moment)
    return pl.pallas_call(
        finish,
        out_shape=(
            jax.ShapeDtypeStruct((ROWS, OWN), F32),
            jax.ShapeDtypeStruct((32, OWN), F32),
            jax.ShapeDtypeStruct((32, OWN), F32),
        ),
        in_specs=[any_] * 5,
        out_specs=[any_] * 3,
        scratch_shapes=[
            vmem((ROWS, OWN), F32), vmem((ROWS, OWN), F32),
            vmem((32, OWN), F32), vmem((32, OWN), F32), vmem((32, OWN), F32),
            dma((11,)), dma((6,)),
        ],
        compiler_params=pltpu.CompilerParams(vmem_limit_bytes=62 * 2**20),
        name="galore_update",
    )(delta, clipped, weight, first_moment, second_moment)


def solution(mesh):
    in_specs = (
        P("dp", "tensor", None),
        P("tensor", None),
        P("tensor", "dp"),
        P("tensor", "dp"),
        P("tensor", "dp"),
    )
    out_specs = (P("tensor", "dp"), P("tensor", "dp"), P("tensor", "dp"))
    return jax.shard_map(body, mesh=mesh, in_specs=in_specs, out_specs=out_specs, check_vma=False)
```

```python
import jax
import jax.numpy as jnp
from jax import lax
from jax.experimental import pallas as pl
from jax.experimental.pallas import tpu as pltpu
from jax.sharding import PartitionSpec as P

FFW = 14336
R = 512
STEP = 10
OWN = 896
LANE = 128
ROWS = 256
NZ = 8
NA = 4
NB = 3
MESH = pl.DeviceIdType.MESH
F32 = jnp.float32
BF16 = jnp.bfloat16


def split(x):
    hi = x.astype(BF16)
    return hi, (x - hi.astype(F32)).astype(BF16)


def dot3(ah, al, bh, bl):
    def mm(a, b):
        return jnp.dot(a, b, preferred_element_type=F32)

    return mm(ah, bh) + (mm(ah, bl) + mm(al, bh))


def kernel(
    g_ref, basis_ref, first_ref, second_ref,
    out_ref, clipped_ref,
    ga, gb, cs, cr, zr, pb, rb1, rb2, rb3, rb4, qr, qz, pa, ah, hs, ar,
    fin, ssq1, ssq2, dirs, delta, m1, m2, bbuf, bth, btl, bh, bl,
    gsem, lsem, fsend, frecv, csend, crecv, zsend, zrecv, asend, arecv,
    bsend, brecv, qsend, qrecv, hsend, hrecv, rsend, rrecv, nsend, nrecv, dsend, drecv,
):
    d = lax.axis_index("dp")
    t = lax.axis_index("tensor")
    z, c = d // 2, d % 2
    y, x = t // 4, t % 4

    def at_z(k):
        return (((z + k + NZ) % NZ) * 2 + c, t)

    def at_x(k):
        return (d, y * 4 + (x + k + 4) % 4)

    def at_y(k):
        return (d, ((y + k + 4) % 4) * 4 + x)

    partner = (z * 2 + 1 - c, t)

    barrier = pltpu.get_barrier_semaphore()

    for to in (at_z(1), at_z(-1), at_x(1), at_x(-1), at_y(1), at_y(-1), partner):
        pl.semaphore_signal(barrier, 1, device_id=to, device_id_type=MESH)

    def gload(group, which, start):
        core = c if which == 0 else 1 - c
        first, last = (1, NZ) if group == 0 else (0, 1) if group == 3 else (0, NZ)
        if group != 2:
            buf, lo, width = ga.at[which, group % 3], 256 * (group % 3), 256
        else:
            buf, lo, width = gb.at[which], NA * LANE, NB * LANE
        sem = gsem.at[group, which]
        if not start:
            part = buf.at[first:last]
            pltpu.make_async_copy(part, part, sem).wait()
            return

        def one(k, _):
            col = pl.multiple_of(OWN * (2 * ((z + 4 + k) % NZ) + core) + lo, LANE)
            pltpu.make_async_copy(g_ref.at[:, pl.ds(col, width)], buf.at[k], sem).start()
            return 0

        lax.fori_loop(first, last, one, 0)

    small = [
        pltpu.make_async_copy(basis_ref, bbuf, lsem.at[0]),
        pltpu.make_async_copy(first_ref, m1, lsem.at[1]),
        pltpu.make_async_copy(second_ref, m2, lsem.at[2]),
    ]
    gload(3, 1, True)
    gload(3, 0, True)
    gload(2, 1, True)
    gload(0, 1, True)
    small[0].start()
    gload(0, 0, True)
    gload(2, 0, True)
    gload(1, 1, True)
    gload(1, 0, True)
    for cp in small[1:]:
        cp.start()

    pending = []

    def remote(src, dst, ssem, rsem, dev):
        cp = pltpu.make_async_remote_copy(
            src_ref=src, dst_ref=dst, send_sem=ssem, recv_sem=rsem,
            device_id=dev, device_id_type=MESH,
        )
        cp.start()
        pending.append(cp)
        return cp

    loaded = set()

    def grad(j, which, k):
        if j < NA:
            return ga[which, j // 2, k, :, (j % 2) * LANE:(j % 2 + 1) * LANE].astype(F32)
        return gb[which, k, :, (j - NA) * LANE:(j - NA + 1) * LANE].astype(F32)

    def need(j, which, far_only=False):
        group = j // 2 if j < NA else 2
        for part in (3,) if far_only and group == 0 else (3, 0) if group == 0 else (group,):
            if (part, which) not in loaded:
                loaded.add((part, which))
                gload(part, which, False)

    core = {}
    far = {}

    def cast(j, lo, hi):
        need(j, 1, hi == 1)

        def one(k, _):
            cs[j, k] = grad(j, 1, k)
            return 0

        lax.fori_loop(lo, hi, one, 0)

    def send_far(j):
        far[j] = remote(cs.at[j, 0], cr.at[j, 0], fsend.at[j], frecv.at[j], partner)

    def send_rest(j):
        core[j] = remote(cs.at[j, 1:NZ], cr.at[j, 1:NZ], csend.at[j], crecv.at[j], partner)

    def stage(j):
        cast(j, 0, NZ)
        if j < NA:
            send_far(j)
            send_rest(j)
        else:
            core[j] = remote(cs.at[j], cr.at[j], csend.at[j], crecv.at[j], partner)

    az = {}
    waited = set()

    def once(table, *keys):
        for key in keys:
            if (id(table), key) not in waited:
                waited.add((id(table), key))
                table[key].wait_recv()

    def a_send(j, s):
        for side, sign in ((0, 1), (1, -1)):
            dest = (4 + sign * (5 - s)) % NZ
            rows = pl.ds(0, ROWS)
            if s == 1:
                rows = pl.ds(128 * side, 128)
            elif s == 2:
                az[j, side, 1].wait_recv()
                half = pl.ds(128 * side, 128)
                cr[j, dest, half] = cr[j, dest, half] + zr[j, side, 0, 0:128]
            else:
                az[j, side, s - 1].wait_recv()
                cr[j, dest] = cr[j, dest] + zr[j, side, s - 2]
            to = zr.at[j, side, 0, 0:128] if s == 1 else zr.at[j, side, s - 1]
            az[j, side, s] = remote(
                cr.at[j, dest, rows], to,
                zsend.at[j, side, s - 1], zrecv.at[j, side, s - 1], at_z(sign))

    def a0(j):
        need(j, 0, True)
        far[j].wait_recv()
        cr[j, 0] = cr[j, 0] + grad(j, 0, 0)
        a_send(j, 1)

    def a1(j):
        need(j, 0)
        core[j].wait_recv()

        def one(k, _):
            cr[j, k] = cr[j, k] + grad(j, 0, k)
            return 0

        lax.fori_loop(1, NZ, one, 0)

    def spread(src, dst, ssem, rsem, peers):
        for k, to in enumerate(peers):
            pltpu.make_async_remote_copy(
                src_ref=src(k + 1), dst_ref=dst.at[k], send_sem=ssem, recv_sem=rsem,
                device_id=to, device_id_type=MESH).start()

    def line(over_x):
        return [at_x(k) if over_x else at_y(k) for k in (1, 2, 3)]

    def a5(j):
        once(az, (j, 0, 4), (j, 1, 4))
        total = cr[j, 4] + zr[j, 0, 3] + zr[j, 1, 3]
        hi, lo = split(total)
        pa[j] = dot3(bth[...], btl[...], hi, lo).reshape(4, 4, 32, LANE)
        if j >= 2:
            spread(
                lambda k: pa.at[j, (t + k) % 16 // 4, (t + k) % 4], ar.at[j],
                asend.at[j], arecv.at[j], [(d, (t + k) % 16) for k in range(1, 16)])
        elif j == 0:
            spread(lambda k: pa.at[j, :, (x + k) % 4], ah.at[j], hsend.at[j], hrecv.at[j], line(True))
        else:
            spread(lambda k: pa.at[j, (y + k) % 4], ah.at[j], hsend.at[j], hrecv.at[j], line(False))

    def a7(j):
        wait_bytes(ah.at[j], hrecv.at[j])
        if j == 0:
            hs[j] = pa[j, :, x] + (ah[j, 0] + ah[j, 1] + ah[j, 2])
            spread(lambda k: hs.at[j, (y + k) % 4], ar.at[j], asend.at[j], arecv.at[j], line(False))
        else:
            hs[j] = pa[j, y] + (ah[j, 0] + ah[j, 1] + ah[j, 2])
            spread(lambda k: hs.at[j, (x + k) % 4], ar.at[j], asend.at[j], arecv.at[j], line(True))

    def wait_bytes(ref, sem):
        pltpu.make_async_copy(ref, ref, sem).wait()

    def a6(j):
        cols = slice(j * LANE, (j + 1) * LANE)
        if j >= 2:
            wait_bytes(ar.at[j], arecv.at[j])
            fin[:, cols] = pa[j, y, x] + jnp.sum(ar[j], axis=0)
        else:
            wait_bytes(ar.at[j, 0:3], arecv.at[j])
            fin[:, cols] = hs[j, y if j == 0 else x] + (ar[j, 0] + ar[j, 1] + ar[j, 2])

    bx = {}

    def piece(j, h, stage_no, k, cols):
        lane = pl.ds(512 * h + cols[0], cols[1])
        if stage_no == 0:
            if h == 0:
                return pb.at[j, :, (x + k + 4) % 4, :, lane]
            return pb.at[j, (y + k + 4) % 4, :, :, lane]
        if h == 0:
            return pb.at[j, (y + k + 4) % 4, x, :, lane]
        return pb.at[j, y, (x + k + 4) % 4, :, lane]

    def toward(h, stage_no, k):
        return at_x(k) if (h + stage_no) % 2 == 0 else at_y(k)

    def b_first(j, stage_no):
        buf = rb1 if stage_no == 0 else rb3
        for h in (0, 1):
            for side, sign in ((0, 1), (1, -1)):
                bx[j, h, side, stage_no, 0] = remote(
                    piece(j, h, stage_no, 2, (256 * side, 256)), buf.at[j, h, side],
                    bsend.at[j, h, side, 2 * stage_no], brecv.at[j, h, side, 2 * stage_no],
                    toward(h, stage_no, sign))

    def b_second(j, stage_no):
        got, buf = (rb1, rb2) if stage_no == 0 else (rb3, rb4)
        for h in (0, 1):
            for side, sign in ((0, 1), (1, -1)):
                bx[j, h, side, stage_no, 0].wait_recv()
                part = piece(j, h, stage_no, sign, (256 * side, 256))
                part[...] = part[...] + got[j, h, side]
                bx[j, h, side, stage_no, 1] = remote(
                    piece(j, h, stage_no, sign, (0, 512)), buf.at[j, h, side],
                    bsend.at[j, h, side, 2 * stage_no + 1], brecv.at[j, h, side, 2 * stage_no + 1],
                    toward(h, stage_no, sign))

    def b_close(j, stage_no):
        buf = rb2 if stage_no == 0 else rb4
        for h in (0, 1):
            once(bx, (j, h, 0, stage_no, 1), (j, h, 1, stage_no, 1))
            part = piece(j, h, stage_no, 0, (0, 512))
            part[...] = part[...] + (buf[j, h, 0] + buf[j, h, 1])

    def b1(j):
        n = NA + j
        need(n, 0)
        core[n].wait_recv()

        def one(q, _):
            total = jnp.concatenate(
                [cr[n, 2 * q] + grad(n, 0, 2 * q), cr[n, 2 * q + 1] + grad(n, 0, 2 * q + 1)], axis=1)
            hi, lo = split(total)
            cols = pl.ds(pl.multiple_of(q * 256, 256), 256)
            pb[j, :, :, :, cols] = dot3(bth[...], btl[...], hi, lo).reshape(4, 4, 32, 256)
            return 0

        lax.fori_loop(0, 4, one, 0)
        b_first(j, 0)

    def b3(j):
        b_close(j, 0)
        b_first(j, 1)

    rx = {}

    def r_send(j, s):
        for side, sign in ((0, 1), (1, -1)):
            dest = (4 + sign * (5 - s)) % NZ
            col = slice(LANE * dest, LANE * (dest + 1))
            rows = slice(0, 32)
            if s <= 2:
                half = slice(16 * side, 16 * side + 16)
            if s == 1:
                rows = half
            else:
                rx[j, side, s - 1].wait_recv()
                if s == 2:
                    pb[j, y, x, half, col] = pb[j, y, x, half, col] + qz[side, 0, 0:16]
                else:
                    pb[j, y, x, :, col] = pb[j, y, x, :, col] + qz[side, s - 2]
            to = qz.at[side, 0, 0:16] if s == 1 else qz.at[side, s - 1]
            rx[j, side, s] = remote(
                pb.at[j, y, x, rows, col], to,
                rsend.at[side, s - 1], rrecv.at[side, s - 1], at_z(sign))

    def b5(j):
        b_close(j, 1)
        if j == 0:
            r_send(j, 1)
            return

        def block(k):
            col = LANE * ((4 + k) % NZ)
            return pb.at[j, y, x, :, col:col + LANE]

        spread(block, qr.at[j], qsend.at[j], qrecv.at[j], [at_z(k) for k in range(1, NZ)])

    def b6(j):
        n = NA + j
        own = pb[j, y, x, :, 4 * LANE:5 * LANE]
        if j == 0:
            rx[j, 0, 4].wait_recv()
            rx[j, 1, 4].wait_recv()
            fin[:, n * LANE:(n + 1) * LANE] = own + (qz[0, 3] + qz[1, 3])
        else:
            wait_bytes(qr.at[j], qrecv.at[j])
            fin[:, n * LANE:(n + 1) * LANE] = own + jnp.sum(qr[j], axis=0)

    def meet(_):
        once(az, (0, 0, 4), (0, 1, 4))
        once(bx, *[(0, h, side, 1, 1) for h in (0, 1) for side in (0, 1)])

    def r2(j):
        r_send(j, 2)

    def r3(j):
        r_send(j, 3)

    def r4(j):
        r_send(j, 4)

    def a2(j):
        a_send(j, 2)

    def a3(j):
        a_send(j, 3)

    def a4(j):
        a_send(j, 4)

    def b2(j):
        b_second(j, 0)

    def b4(j):
        b_second(j, 1)

    firsts = (0, -1, 1, 2)
    sides = ((0, 1), (1, -1))

    def gather(buf):
        dx = {}

        def send(h, ring, hop, n, side, first, second, part):
            yo, xo = (second, first) if h == 0 else (first, second)
            ref = buf.at[(y + yo + 4) % 4, (x + xo + 4) % 4, pl.ds(16 * h + part[0], part[1])]
            dx[h, ring, hop, n, side] = remote(
                ref, ref, dsend.at[h, ring, hop, n, side], drecv.at[h, ring, hop, n, side],
                toward(h, ring, sides[side][1]))

        def own():
            for ring in (0, 1):
                for h in (0, 1):
                    for side, _ in sides:
                        send(h, ring, 0, 0, side, 0, 0, (0, 16))

        def first_halves():
            for side, sign in sides:
                for h in (0, 1):
                    dx[h, 0, 0, 0, side].wait_recv()
                    send(h, 0, 1, 0, side, -sign, 0, (8 * side, 8))

        def second(n):
            for h in (0, 1):
                if n == 3:
                    for side, _ in sides:
                        dx[h, 0, 1, 0, side].wait_recv()
                for side, _ in sides:
                    send(h, 1, 0, n, side, firsts[n], 0, (0, 16))

        def second_halves(n):
            for h in (0, 1):
                for side, sign in sides:
                    dx[h, 1, 0, n, side].wait_recv()
                    send(h, 1, 1, n, side, firsts[n], -sign, (8 * side, 8))

        def close():
            for n in range(4):
                for h in (0, 1):
                    for side, _ in sides:
                        dx[h, 1, 1, n, side].wait_recv()

        return own, first_halves, second, second_halves, close

    cast(0, 0, 1)
    cast(1, 0, 1)
    pl.semaphore_wait(barrier, 7)
    send_far(0)
    send_far(1)
    stage(4)

    def rest(j):
        cast(j, 1, NZ)
        send_rest(j)

    def prep(_):
        small[0].wait()
        hi, lo = split(bbuf[...].T)
        bth[...] = hi
        btl[...] = lo

    def flush(_):
        for cp in pending:
            cp.wait_send()
        pending.clear()
        for cp in small[1:]:
            cp.wait()
        hi, lo = split(bbuf[...])
        bh[...] = hi
        bl[...] = lo

    order = (
        (rest, 1), (stage, 5), (a0, 1), (a0, 0), (rest, 0), (stage, 3), (prep, 0), (b1, 0), (a1, 1), (a2, 1),
        (stage, 6), (b1, 1), (a1, 0), (a2, 0), (stage, 2), (a1, 3), (b2, 0), (a0, 2), (a0, 3), (b1, 2),
        (a1, 2), (a3, 0), (a2, 2), (a3, 1), (a2, 3), (b3, 0), (b2, 1), (b2, 2), (a3, 2), (b4, 0), (a4, 0),
        (b3, 1), (a4, 2), (a3, 3), (b3, 2), (meet, 0), (b5, 0), (a4, 1), (b4, 1), (a5, 2), (b4, 2), (a5, 0),
        (r2, 0), (a4, 3), (a5, 1), (r3, 0), (b5, 1), (b5, 2), (a6, 2), (a5, 3), (r4, 0), (a7, 0), (a7, 1),
        (b6, 1), (b6, 0), (a6, 1), (a6, 0), (flush, 0), (a6, 3), (b6, 2),
    )
    for step, j in order:
        step(j)

    acc = jnp.zeros((8, LANE), F32)
    for r in range(4):
        for j in range(7):
            v = fin[8 * r:8 * r + 8, LANE * j:LANE * (j + 1)]
            acc = acc + v * v

    ssq1[15] = acc
    spread(lambda k: ssq1.at[15], ssq1, nsend.at[0], nrecv.at[0], [((d + k) % 16, t) for k in range(1, 16)])
    wait_bytes(ssq1.at[0:15], nrecv.at[0])
    ssq2[15] = jnp.sum(ssq1[...], axis=0)
    spread(lambda k: ssq2.at[15], ssq2, nsend.at[1], nrecv.at[1], [(d, (t + k) % 16) for k in range(1, 16)])
    wait_bytes(ssq2.at[0:15], nrecv.at[1])
    squares = jnp.sum(jnp.sum(ssq2[...], axis=0), axis=0, keepdims=True)
    squares = jnp.sum(squares, axis=1, keepdims=True)
    limit = 0.25 * (R * FFW) ** 0.5
    factor = jnp.minimum(jnp.float32(1.0), limit / (jnp.sqrt(squares) + 1e-06))

    clipped = factor * fin[...]
    new_first = 0.9 * m1[...] + 0.1 * clipped
    new_second = 0.95 * m2[...] + 0.05 * clipped * clipped
    dirs[y, x] = new_first / (1.0 - 0.9**STEP) / (jnp.sqrt(new_second / (1.0 - 0.95**STEP)) + 1e-08)
    own, first_halves, second, second_halves, close = gather(dirs)
    own()
    fin[...] = clipped
    outs = [pltpu.make_async_copy(fin, clipped_ref, lsem.at[0])]
    outs[0].start()

    first_halves()
    for n in (1, 2, 3):
        second(n)
    for n in (0, 1, 2):
        second_halves(n)
    for j in (0, 1):
        wait_bytes(ah.at[j], hsend.at[j])
        wait_bytes(ar.at[j, 0:3], asend.at[j])
    for j in (2, 3):
        wait_bytes(ar.at[j], asend.at[j])
    for j in (1, 2):
        wait_bytes(qr.at[j], qsend.at[j])
    wait_bytes(ssq1.at[0:15], nsend.at[0])
    wait_bytes(ssq2.at[0:15], nsend.at[1])
    second_halves(3)
    close()
    for n, (lo_col, width) in enumerate(((0, 256), (256, 256), (512, 256), (768, 128))):
        cols = slice(lo_col, lo_col + width)
        hi, lo = split(dirs[:, :, :, cols].reshape(R, width))
        delta[:, cols] = dot3(bh[...], bl[...], hi, lo)
        outs.append(pltpu.make_async_copy(delta.at[:, cols], out_ref.at[:, cols], lsem.at[1 + n]))
        outs[-1].start()
    for cp in pending:
        cp.wait_send()
    for cp in outs:
        cp.wait()


def finish(
    delta_ref, clipped_ref, weight_ref, first_ref, second_ref,
    out_ref, out_first_ref, out_second_ref,
    dbuf, wbuf, clipped, m1, m2, sem, osem,
):
    loads = [
        pltpu.make_async_copy(clipped_ref, clipped, sem.at[8]),
        pltpu.make_async_copy(first_ref, m1, sem.at[9]),
        pltpu.make_async_copy(second_ref, m2, sem.at[10]),
    ]
    for n in range(4):
        rows = pl.ds(64 * n, 64)
        loads.append(pltpu.make_async_copy(weight_ref.at[rows], wbuf.at[rows], sem.at[2 * n]))
        loads.append(pltpu.make_async_copy(delta_ref.at[rows], dbuf.at[rows], sem.at[2 * n + 1]))
    for cp in loads:
        cp.start()
    for cp in loads[0:3]:
        cp.wait()
    m1[...] = 0.9 * m1[...] + 0.1 * clipped[...]
    m2[...] = 0.95 * m2[...] + 0.05 * clipped[...] * clipped[...]
    outs = [
        pltpu.make_async_copy(m1, out_first_ref, osem.at[4]),
        pltpu.make_async_copy(m2, out_second_ref, osem.at[5]),
    ]
    for cp in outs:
        cp.start()
    for n in range(4):
        rows = slice(64 * n, 64 * n + 64)
        loads[3 + 2 * n].wait()
        loads[4 + 2 * n].wait()
        wbuf[rows] = wbuf[rows] - 0.5 * dbuf[rows]
        outs.append(pltpu.make_async_copy(wbuf.at[rows], out_ref.at[rows], osem.at[n]))
        outs[-1].start()
    for cp in outs:
        cp.wait()


def body(grads, basis, weight, first_moment, second_moment):
    dma = pltpu.SemaphoreType.DMA
    vmem = pltpu.VMEM
    any_ = pl.BlockSpec(memory_space=pl.ANY)
    delta, clipped = pl.pallas_call(
        kernel,
        out_shape=(
            jax.ShapeDtypeStruct((ROWS, OWN), F32),
            jax.ShapeDtypeStruct((32, OWN), F32),
        ),
        in_specs=[any_] * 4,
        out_specs=[any_] * 2,
        scratch_shapes=[
            vmem((2, 2, NZ, ROWS, 256), BF16),
            vmem((2, NZ, ROWS, NB * LANE), BF16),
            vmem((NA + NB, NZ, ROWS, LANE), F32),
            vmem((NA + NB, NZ, ROWS, LANE), F32),
            vmem((NA, 2, 4, ROWS, LANE), F32),
            vmem((NB, 4, 4, 32, 1024), F32),
            vmem((NB, 2, 2, 4, 32, 256), F32),
            vmem((NB, 2, 2, 4, 32, 512), F32),
            vmem((NB, 2, 2, 32, 256), F32),
            vmem((NB, 2, 2, 32, 512), F32),
            vmem((NB, NZ - 1, 32, LANE), F32),
            vmem((2, 4, 32, LANE), F32),
            vmem((NA, 4, 4, 32, LANE), F32),
            vmem((2, 3, 4, 32, LANE), F32),
            vmem((2, 4, 32, LANE), F32),
            vmem((NA, 15, 32, LANE), F32),
            vmem((32, OWN), F32),
            vmem((16, 8, LANE), F32),
            vmem((16, 8, LANE), F32),
            vmem((4, 4, 32, OWN), F32),
            vmem((ROWS, OWN), F32),
            vmem((32, OWN), F32),
            vmem((32, OWN), F32),
            vmem((ROWS, R), F32),
            vmem((R, ROWS), BF16),
            vmem((R, ROWS), BF16),
            vmem((ROWS, R), BF16),
            vmem((ROWS, R), BF16),
            dma((4, 2)),
            dma((5,)),
            dma((NA,)), dma((NA,)),
            dma((NA + NB,)), dma((NA + NB,)),
            dma((NA, 2, 4)), dma((NA, 2, 4)),
            dma((NA,)), dma((NA,)),
            dma((NB, 2, 2, 4)), dma((NB, 2, 2, 4)),
            dma((NB,)), dma((NB,)),
            dma((2,)), dma((2,)),
            dma((2, 4)), dma((2, 4)),
            dma((2,)), dma((2,)),
            dma((2, 2, 2, 4, 2)), dma((2, 2, 2, 4, 2)),
        ],
        compiler_params=pltpu.CompilerParams(
            collective_id=0, has_side_effects=True, vmem_limit_bytes=62 * 2**20),
        name="galore_step",
    )(grads[0], basis, first_moment, second_moment)
    return pl.pallas_call(
        finish,
        out_shape=(
            jax.ShapeDtypeStruct((ROWS, OWN), F32),
            jax.ShapeDtypeStruct((32, OWN), F32),
            jax.ShapeDtypeStruct((32, OWN), F32),
        ),
        in_specs=[any_] * 5,
        out_specs=[any_] * 3,
        scratch_shapes=[
            vmem((ROWS, OWN), F32), vmem((ROWS, OWN), F32),
            vmem((32, OWN), F32), vmem((32, OWN), F32), vmem((32, OWN), F32),
            dma((11,)), dma((6,)),
        ],
        compiler_params=pltpu.CompilerParams(vmem_limit_bytes=62 * 2**20),
        name="galore_update",
    )(delta, clipped, weight, first_moment, second_moment)


def solution(mesh):
    in_specs = (
        P("dp", "tensor", None),
        P("tensor", None),
        P("tensor", "dp"),
        P("tensor", "dp"),
        P("tensor", "dp"),
    )
    out_specs = (P("tensor", "dp"), P("tensor", "dp"), P("tensor", "dp"))
    return jax.shard_map(body, mesh=mesh, in_specs=in_specs, out_specs=out_specs, check_vma=False)
```
